128 devices in a mesh: region: 4 (over z), rays: 32 (over x, y, core).
Axes of the slice: x: 4, y: 4, z: 4, core: 2. Of those that a mesh axis runs over, the one named last changes fastest.
Arguments:
- tile_values: float32 [32768, 128, 128], P(('region', 'rays')), may hold values from -0.1875 to 0.1875
- tile_row: int32 [32768], P(('region', 'rays')), may hold values from 0 to 15
- tile_owner: int32 [32768, 1], P(('region', 'rays')), may hold values from 0 to 127; in each aligned block of 256 rows (0 to 255, 256 to 511, ...) at most 2 rows name the same one
- tile_sub: int32 [32768], P(('region', 'rays')), may hold values from 0 to 31
- tile_count: int32 [128], P(('region', 'rays')), may hold values from 128 to 256, as said below
- residual_times: float32 [4, 262144], P(None, ('region', 'rays')), may hold values from -16 to 16
Outputs:
- slowness_update: float32 [4, 524288], P(None, ('region', 'rays'))
- relative_residual: float32 [4], replicated
The draws below stay inside these ranges and needn't reach their ends.
Inputs may be any that keep to these rules, and one draw needn't show every extreme that they name: `tile_owner`: among the 256 entries of one device, at most 2 name one owner. `tile_count`: each count is 256 or 128, and some device has all 256.
All inputs are finite; a program needn't handle non-finite values.
Results may differ from the reference program's by a relative error of at most 0.0003.
Values sent between devices are 32-bit elements; how exact they have to be, the bound alone decides.
A program may use at most 64 MiB of HBM per device.

```python
import math
import jax
import jax.numpy as jnp
import numpy as np
from jax import lax

TB = 128
TILES = 256
RB = 16
CB = 32
NRHS = 4
ITERS = 2
OWNERS = 128
SLOTS = 2
RAYS = 262144
CELLS = 524288


def draw_tile_count(key, part):
    key = jax.random.fold_in(key, 23)
    first_key, second_key = jax.random.split(key)
    shifts = jax.random.randint(first_key, (OWNERS,), 0, 2).astype(jnp.int32)
    divisors = jnp.left_shift(jnp.ones((OWNERS,), jnp.int32), shifts)
    counts = (TILES // divisors).astype(jnp.int32)
    busiest = jax.random.randint(second_key, (), 0, OWNERS)
    return counts.at[busiest].set(TILES).astype(jnp.int32)


def draw_residual_times(key, part):
    key = jax.random.fold_in(key, 11)
    position = jnp.arange(RAYS, dtype=jnp.float32) / RAYS
    rising = jnp.exp(jnp.log(3.0) * position)
    values = jnp.clip(jax.random.normal(key, (NRHS, RAYS), jnp.float32), -4.0, 4.0) * rising[None, :]
    return values.astype(jnp.float32)


def touch_ends(result, own_key, least, top_value):
    longest = result.shape.index(max(result.shape))
    spots = []
    for shift in (0, 1):
        where = [jax.random.randint(jax.random.fold_in(own_key, axis), (), 0, length) for axis, length in enumerate(result.shape)]
        where[longest] = (where[longest] + shift) % result.shape[longest]
        spots.append(tuple(where))
    return result.at[spots[0]].set(least).at[spots[1]].set(top_value)


def levels(stream_key, shape, pieces, low, top_value):
    def one(dim, shards_of):
        steps = jax.random.uniform(jax.random.fold_in(jax.random.fold_in(stream_key, 6), dim), (shards_of,), jnp.float32, low / len(pieces), top_value / len(pieces))
        return jnp.repeat(jnp.exp(steps), shape[dim] // shards_of).reshape((-1,) + (1,) * (len(shape) - dim - 1))

    gain = one(*pieces[0])
    for cut in pieces[1:]:
        gain = gain * one(*cut)
    return gain


def routed_block(own_key, own, number, rows, count, top, bound, skew):
    order = jax.random.permutation(own_key, count)
    heavy_load, common = load_shares(count, rows * top, bound, skew, True), load_shares(count, rows * top, bound, skew, False)
    places = jnp.arange(count)

    def named(lengths, rotation):
        used = int((lengths > 0).sum())
        fixed = max(1, used // 4)
        passed = fixed + (places - fixed + rotation * (used - fixed)) % max(1, count - fixed)
        return jnp.zeros((count,), jnp.int32).at[order[jnp.where(places < fixed, places, passed)]].set(jnp.asarray(lengths, jnp.int32))

    lengths = jnp.where(number % 4 == 0, named(heavy_load, number // 4), named(common, number - number // 4 - 1))
    mixed = jax.random.permutation(jax.random.fold_in(own, 3), count)
    source_of, taker = mixed[0:count // 2 * 2:2], mixed[1:count // 2 * 2:2]
    room = jnp.minimum(lengths[source_of] - 1, bound - lengths[taker]) // 2
    room = jnp.where((source_of == order[0]) | (taker == order[0]) | (lengths[taker] == 0), 0, jnp.maximum(room, 0))
    passed = jax.random.randint(jax.random.fold_in(own, 4), (count // 2,), 0, 1 << 20) % (room + 1)
    lengths = lengths.at[source_of].add(-passed).at[taker].add(passed)
    labels = jnp.searchsorted(jnp.cumsum(lengths), jnp.arange(rows * top), side="right").astype(jnp.int32)
    grid = labels.reshape(top, rows).T
    grid = grid[jax.random.permutation(jax.random.fold_in(own, 1), rows)]
    rotation = jax.random.randint(jax.random.fold_in(own, 2), (rows, 1), 0, top)
    return jnp.take_along_axis(grid, (jnp.arange(top)[None, :] + rotation) % top, axis=1)


def load_shares(amount, total, bound, slope, full):
    loads = [(1 << 20) // math.isqrt(rank ** slope) + 1 for rank in range(1, amount + 1)]
    largest = bound if full else min(bound, max(-(-total // amount), total * loads[0] // sum(loads)))
    least = 1 if total - largest >= amount - 1 else 0
    given, surplus = [largest] + [least] * (amount - 1), total - largest - least * (amount - 1)
    while surplus > 0:
        free = [i for i in range(1, amount) if given[i] < largest] or [i for i in range(1, amount) if given[i] < bound]
        mass, left = sum([loads[i] for i in free]), surplus
        for i in free:
            more = min(bound - given[i], max(1, left * loads[i] // mass), surplus)
            given[i] = given[i] + more
            surplus = surplus - more
    return np.array(given)


def noise(stream_key, extent, spread, reach, pieces=(), held_as=jnp.bfloat16):
    gain = levels(stream_key, extent, pieces, -0.22, 0.18) if pieces else 1.0
    array = jax.random.normal(stream_key, extent, jnp.float32) * spread * gain
    return jnp.minimum(jnp.maximum(array, -reach), reach).astype(held_as)


def setup_inputs(seed: int = 0) -> dict:
    arg_keys = jax.random.split(jax.random.key(seed), 7)
    tile_values = noise(arg_keys[0], (OWNERS * TILES, TB, TB), (TB * TILES // (2 * RB)) ** -0.5, 0.1875, ((0, 128),), jnp.float32)
    tile_row = touch_ends(jax.random.randint(arg_keys[1], (OWNERS * TILES,), 0, RB), jax.random.fold_in(arg_keys[1], 1), 0, RB - 1).astype(jnp.int32)
    tile_owner_keys = jax.random.split(jax.random.fold_in(arg_keys[2], 1), (OWNERS * TILES) // TILES)
    tile_owner_turns = jax.random.permutation(jax.random.fold_in(arg_keys[2], 3), (OWNERS * TILES) // TILES)
    tile_owner = jax.vmap(lambda own, number: routed_block(jax.random.fold_in(arg_keys[2], 2), own, number, TILES, OWNERS, 1, SLOTS, 2))(tile_owner_keys, tile_owner_turns).reshape((OWNERS * TILES, 1))
    tile_sub = touch_ends(jax.random.randint(arg_keys[3], (OWNERS * TILES,), 0, CB), jax.random.fold_in(arg_keys[3], 1), 0, CB - 1).astype(jnp.int32)
    tile_count = draw_tile_count(jax.random.fold_in(arg_keys[6], 71), 0)
    residual_times = draw_residual_times(jax.random.fold_in(arg_keys[6], 71), 0)
    return {"tile_values": tile_values, "tile_row": tile_row, "tile_owner": tile_owner, "tile_sub": tile_sub, "tile_count": tile_count, "residual_times": residual_times}


EPSILON = 1e-06
PRECISE = lax.Precision.HIGHEST

def layout(tile_row, tile_owner, tile_sub, tile_count):
    total = tile_row.shape[0]
    tile_index = jnp.arange(total, dtype=jnp.int32)
    device = tile_index // TILES
    row_block = (device * RB + tile_row).astype(jnp.int32)
    column_block = (tile_owner[:, 0] * CB + tile_sub).astype(jnp.int32)
    live_mask = (tile_index % TILES < tile_count[device]).astype(jnp.float32)
    return (row_block, column_block, live_mask)

def forward(tile_values, row_block, column_block, live_mask, model_vec):
    blocks = model_vec.reshape(NRHS, CB * OWNERS, TB).transpose(1, 0, 2)
    picked = blocks[column_block] * live_mask[:, None, None]
    products = jnp.einsum('trc,tnc->tnr', tile_values, picked, precision=PRECISE)
    summed = jax.ops.segment_sum(products, row_block, num_segments=RB * OWNERS)
    return summed.transpose(1, 0, 2).reshape(NRHS, RAYS)

def adjoint(tile_values, row_block, column_block, live_mask, ray_vec):
    blocks = ray_vec.reshape(NRHS, RB * OWNERS, TB).transpose(1, 0, 2)
    picked = blocks[row_block] * live_mask[:, None, None]
    products = jnp.einsum('trc,tnr->tnc', tile_values, picked, precision=PRECISE)
    summed = jax.ops.segment_sum(products, column_block, num_segments=CB * OWNERS)
    return summed.transpose(1, 0, 2).reshape(NRHS, CELLS)

def norm_of(values):
    return jnp.sqrt(lax.optimization_barrier(jnp.sum(values * values, axis=1)) + EPSILON)

def reference(tile_values, tile_row, tile_owner, tile_sub, tile_count, residual_times):
    row_block, column_block, live_mask = layout(tile_row, tile_owner, tile_sub, tile_count)
    beta_now = norm_of(residual_times)
    beta_first = beta_now
    ray_vec = residual_times / beta_now[:, None]
    pushed = adjoint(tile_values, row_block, column_block, live_mask, ray_vec)
    alpha_now = norm_of(pushed)
    model_vec = pushed / alpha_now[:, None]
    direction = model_vec
    solution = jnp.zeros((NRHS, CELLS), jnp.float32)
    phi_bar = beta_now
    rho_bar = alpha_now
    for step_index in range(ITERS):
        image_rays = forward(tile_values, row_block, column_block, live_mask, model_vec) - alpha_now[:, None] * ray_vec
        beta_now = norm_of(image_rays)
        ray_vec = image_rays / beta_now[:, None]
        rho_now = jnp.sqrt(rho_bar * rho_bar + beta_now * beta_now)
        cosine = rho_bar / rho_now
        sine_value = beta_now / rho_now
        phi_now = cosine * phi_bar
        phi_bar = sine_value * phi_bar
        solution = solution + (phi_now / rho_now)[:, None] * direction
        if step_index + 1 < ITERS:
            pushed = adjoint(tile_values, row_block, column_block, live_mask, ray_vec) - beta_now[:, None] * model_vec
            alpha_now = norm_of(pushed)
            model_vec = pushed / alpha_now[:, None]
            theta_now = sine_value * alpha_now
            rho_bar = -cosine * alpha_now
            direction = model_vec - (theta_now / rho_now)[:, None] * direction
    return (solution, phi_bar / beta_first)
```

```python
import functools

import jax
import jax.numpy as jnp
from jax import lax
from jax.experimental import pallas as pl
from jax.experimental.pallas import tpu as pltpu
from jax.sharding import PartitionSpec as P

EPSILON = 1e-06
MESH = pl.DeviceIdType.MESH
F32 = jnp.float32
BF16 = jnp.bfloat16

DEVICES = 128
GROUP = 16
GROUPS = DEVICES // GROUP
STRIDE = 37
UNSTRIDE = pow(STRIDE, -1, DEVICES)
NORMS = 5
LOADS = 8


def my_place():
    z = lax.axis_index("region")
    rays = lax.axis_index("rays")
    return z, rays // 8, (rays // 2) % 4, rays % 2


def partner(k, sign=1):
    z, x, y, c = my_place()
    shift = (k * STRIDE) % DEVICES
    oz = (z + 4 + sign * (shift // 32)) % 4
    ox = (x + 4 + sign * ((shift // 8) % 4)) % 4
    oy = (y + 4 + sign * ((shift // 2) % 4)) % 4
    oc = (c + shift % 2) % 2
    return (oz, ox * 8 + oy * 2 + oc)


def split(values):
    high = values.astype(BF16)
    low = (values - high.astype(F32)).astype(BF16)
    return high, low


def dot(a, b):
    return jnp.dot(a, b, preferred_element_type=F32)


def dot_t(a, b):
    return lax.dot_general(a, b, (((1,), (1,)), ((), ())), preferred_element_type=F32)


def kernel(
    order_ref,
    tiles_ref,
    ids_ref,
    rows_ref,
    times_ref,
    update_ref,
    residual_ref,
    tiles,
    weights,
    ids_in,
    outbox,
    inbox,
    cell_pick,
    cell_sum,
    row_pick,
    row_sum,
    spread,
    prods,
    norm_a,
    norm_b,
    norm_mine,
    load_sem,
    id_send,
    id_recv,
    send_sem,
    recv_sem,
    na_send,
    na_recv,
    nb_send,
    nb_recv,
):
    z, x, y, c = my_place()
    xy = x * 4 + y
    zc = z * 2 + c
    per_load = tiles_ref.shape[0] // LOADS

    def load(i):
        where = pl.ds(i * per_load, per_load)
        return pltpu.make_async_copy(tiles_ref.at[where], tiles.at[where], load_sem.at[i])

    for i in range(LOADS):
        load(i).start()

    barrier = pltpu.get_barrier_semaphore()

    def greet(k, carry):
        pl.semaphore_signal(barrier, inc=1, device_id=partner(k), device_id_type=MESH)
        return carry

    lax.fori_loop(1, DEVICES, greet, 0)
    pl.semaphore_wait(barrier, DEVICES - 1)

    def send_id(k, carry):
        pltpu.make_async_remote_copy(
            src_ref=ids_ref.at[k],
            dst_ref=ids_in.at[k],
            send_sem=id_send,
            recv_sem=id_recv,
            device_id=partner(k),
            device_id_type=MESH,
        ).start()
        return carry

    lax.fori_loop(1, DEVICES, send_id, 0)
    ids_in[0] = ids_ref[0]

    def norm_start(turn, part):
        norm_mine[turn, 0] = part
        norm_a[turn, xy] = part

        def one(d, carry):
            ox = (x + d // 4) % 4
            oy = (y + d % 4) % 4
            pltpu.make_async_remote_copy(
                src_ref=norm_mine.at[turn, 0],
                dst_ref=norm_a.at[turn, xy],
                send_sem=na_send.at[turn],
                recv_sem=na_recv.at[turn],
                device_id=(z, ox * 8 + oy * 2 + c),
                device_id_type=MESH,
            ).start()
            return carry

        lax.fori_loop(1, 16, one, 0)

    def norm_middle(turn):
        got = norm_a.at[turn, pl.ds(0, 15)]
        pltpu.make_async_copy(got, got, na_recv.at[turn]).wait()
        total = norm_a[turn, 0]
        for i in range(1, 16):
            total = total + norm_a[turn, i]
        norm_mine[turn, 1] = total
        norm_b[turn, zc] = total

        def one(d, carry):
            oz = (z + d // 2) % 4
            oc = (c + d % 2) % 2
            pltpu.make_async_remote_copy(
                src_ref=norm_mine.at[turn, 1],
                dst_ref=norm_b.at[turn, zc],
                send_sem=nb_send.at[turn],
                recv_sem=nb_recv.at[turn],
                device_id=(oz, x * 8 + y * 2 + oc),
                device_id_type=MESH,
            ).start()
            return carry

        lax.fori_loop(1, 8, one, 0)

    def norm_end(turn):
        got = norm_b.at[turn, pl.ds(0, 7)]
        pltpu.make_async_copy(got, got, nb_recv.at[turn]).wait()
        total = norm_b[turn, 0]
        for i in range(1, 8):
            total = total + norm_b[turn, i]
        total = total + pltpu.roll(total, 4, 0)
        total = jnp.broadcast_to(jnp.sum(total, axis=1, keepdims=True), total.shape)
        return jnp.sqrt(total + EPSILON)

    def norm_part(values):
        squares = (values * values).reshape(-1, 8, 128)
        return jnp.sum(squares, axis=0)

    def tall(scalar, values):
        return jnp.broadcast_to(scalar[None], (values.shape[0] // 8, 8, 128)).reshape(values.shape)

    def group_send(turn, g, sign):
        def one(k, carry):
            @pl.when(k > 0)
            def _():
                pltpu.make_async_remote_copy(
                    src_ref=outbox.at[turn, k],
                    dst_ref=inbox.at[turn, k],
                    send_sem=send_sem.at[turn],
                    recv_sem=recv_sem.at[turn, g],
                    device_id=partner(k, sign),
                    device_id_type=MESH,
                ).start()

            return carry

        lax.fori_loop(g * GROUP, (g + 1) * GROUP, one, 0)

        @pl.when(g == 0)
        def _():
            inbox[turn, 0] = outbox[turn, 0]

    def group_wait(turn, g):
        @pl.when(g == 0)
        def _():
            got = inbox.at[turn, pl.ds(0, GROUP - 1)]
            pltpu.make_async_copy(got, got, recv_sem.at[turn, 0]).wait()

        @pl.when(g > 0)
        def _():
            got = inbox.at[turn, pl.ds(0, GROUP)]
            pltpu.make_async_copy(got, got, recv_sem.at[turn, g]).wait()

    first_half = (lax.broadcasted_iota(jnp.int32, (16, 128), 0) % 8) < 4
    first_rows = lax.broadcasted_iota(jnp.int32, (8, 128), 0) < 4

    def adjoint_send(turn, ray_vec, build):
        high, low = split(ray_vec)
        zero = jnp.zeros((64, 256), BF16)
        source = jnp.concatenate([jnp.concatenate([high, low], axis=1), zero], axis=0)

        def group(g, carry):
            here = pl.ds(g * 128, 128)
            spread[...] = dot(row_pick[here, :], source)
            for i in range(GROUP):
                k = g * GROUP + i
                if build:
                    for s in range(2):
                        tile = tiles[order_ref[2 * k + s]]
                        tile_high, tile_low = split(tile)
                        weights[k, s * 128 : (s + 1) * 128, 0:128] = tile_high
                        weights[k, s * 128 : (s + 1) * 128, 128:256] = tile_low
                both = jnp.concatenate(
                    [spread[i * 8 : i * 8 + 8, 0:128], spread[i * 8 : i * 8 + 8, 128:256]], axis=0
                )
                left = jnp.concatenate(
                    [jnp.where(first_half, both, 0.0), jnp.where(first_half, 0.0, both)], axis=1
                ).astype(BF16)
                out = dot(left, weights[k])
                out = out[:, 0:128] + out[:, 128:256]
                outbox[turn, k] = out[0:8] + out[8:16]
            group_send(turn, g, 1)

            @pl.when(g == 2)
            def _():
                norm_middle(turn)

            return carry

        lax.fori_loop(0, GROUPS, group, 0)

    def adjoint_finish(turn):
        def group(g, total):
            group_wait(turn, g)
            here = pl.multiple_of(g * 128, 128)
            arrived = inbox[turn, pl.ds(g * GROUP, GROUP)].reshape(128, 128)
            high, low = split(arrived)
            sums = cell_sum[g]
            return total + dot(
                jnp.concatenate([sums, sums], axis=1), jnp.concatenate([high, low], axis=0)
            )

        return lax.fori_loop(0, GROUPS, group, jnp.zeros((128, 128), F32))

    def forward_send(turn, model_vec):
        high, low = split(model_vec)
        source = jnp.concatenate([high, low], axis=0)

        def group(g, carry):
            picks = cell_pick[pl.ds(g * 128, 128), :]
            reply = dot(jnp.concatenate([picks, picks], axis=1), source)
            outbox[turn, pl.ds(g * GROUP, GROUP)] = reply.reshape(GROUP, 8, 128)
            group_send(turn, g, -1)
            return carry

        lax.fori_loop(0, GROUPS, group, 0)

    def forward_finish(turn):
        def group(g, total):
            group_wait(turn, g)
            for i in range(GROUP):
                k = g * GROUP + i
                high, low = split(inbox[turn, k])
                both = jnp.concatenate([high.astype(F32), low.astype(F32)], axis=0)
                left = jnp.concatenate([both, both], axis=1).astype(BF16)
                out = dot_t(left, weights[k])
                out = out[0:8] + out[8:16]
                prods[i * 8 : i * 8 + 8, :] = jnp.where(first_rows, out[:, 0:128], out[:, 128:256])
            high, low = split(prods[...])
            sums = row_sum[g]

            @pl.when(g == 0)
            def _():
                norm_middle(turn)

            return total + dot(
                jnp.concatenate([sums, sums], axis=1), jnp.concatenate([high, low], axis=0)
            )

        return lax.fori_loop(0, GROUPS, group, jnp.zeros((128, 128), F32))[0:64]

    data = jnp.concatenate([times_ref[:, b * 128 : (b + 1) * 128] for b in range(16)], axis=0)

    norm_start(0, norm_part(data))
    lanes = lax.broadcasted_iota(jnp.int32, (128, 128), 1)

    def row_marks(g, carry):
        marks = (rows_ref[pl.ds(g * 128, 128), :] == lanes).astype(F32)
        row_pick[pl.ds(g * 128, 128), :] = marks.astype(BF16)
        row_sum[g] = marks.T.astype(BF16)
        return carry

    lax.fori_loop(0, GROUPS, row_marks, 0)
    for i in range(LOADS):
        load(i).wait()

    adjoint_send(0, data, True)

    got_ids = ids_in.at[pl.ds(0, DEVICES - 1)]
    pltpu.make_async_copy(got_ids, got_ids, id_recv).wait()

    def cell_marks(g, carry):
        marks = ids_in[pl.ds(g * GROUP, GROUP)].reshape(128, 128) == lanes
        marks = marks.astype(F32)
        cell_pick[pl.ds(g * 128, 128), :] = marks.astype(BF16)
        cell_sum[g] = marks.T.astype(BF16)
        return carry

    lax.fori_loop(0, GROUPS, cell_marks, 0)

    pushed = adjoint_finish(0)
    beta_first = norm_end(0)
    ray_vec = data / tall(beta_first, data)
    pushed = pushed / tall(beta_first, pushed)

    norm_start(1, norm_part(pushed))
    forward_send(1, pushed)
    image = forward_finish(1)
    alpha = norm_end(1)
    model_vec = pushed / tall(alpha, pushed)
    direction = model_vec
    phi_bar = beta_first
    rho_bar = alpha
    image = image / tall(alpha, image) - tall(alpha, image) * ray_vec

    norm_start(2, norm_part(image))
    adjoint_send(2, image, False)
    pushed = adjoint_finish(2)
    beta = norm_end(2)
    ray_vec = image / tall(beta, image)
    pushed = pushed / tall(beta, pushed) - tall(beta, pushed) * model_vec

    norm_start(3, norm_part(pushed))
    forward_send(3, pushed)
    rho = jnp.sqrt(rho_bar * rho_bar + beta * beta)
    cosine = rho_bar / rho
    sine = beta / rho
    phi = cosine * phi_bar
    phi_bar = sine * phi_bar
    update = tall(phi / rho, direction) * direction
    image = forward_finish(3)
    alpha = norm_end(3)
    model_vec = pushed / tall(alpha, pushed)
    theta = sine * alpha
    rho_bar = -cosine * alpha
    direction = model_vec - tall(theta / rho, direction) * direction
    image = image / tall(alpha, image) - tall(alpha, image) * ray_vec

    norm_start(4, norm_part(image))
    norm_middle(4)
    beta = norm_end(4)
    rho = jnp.sqrt(rho_bar * rho_bar + beta * beta)
    cosine = rho_bar / rho
    sine = beta / rho
    phi = cosine * phi_bar
    phi_bar = sine * phi_bar
    update = update + tall(phi / rho, direction) * direction
    for b in range(32):
        update_ref[:, b * 128 : (b + 1) * 128] = update[b * 4 : b * 4 + 4, :]
    residual_ref[...] = phi_bar / beta_first

    sent = ids_in.at[pl.ds(0, DEVICES - 1)]
    pltpu.make_async_copy(sent, sent, id_send).wait()
    for turn in range(4):
        sent = outbox.at[turn, pl.ds(0, DEVICES - 1)]
        pltpu.make_async_copy(sent, sent, send_sem.at[turn]).wait()
    for turn in range(NORMS):
        sent = norm_a.at[turn, pl.ds(0, 15)]
        pltpu.make_async_copy(sent, sent, na_send.at[turn]).wait()
        sent = norm_b.at[turn, pl.ds(0, 7)]
        pltpu.make_async_copy(sent, sent, nb_send.at[turn]).wait()


def plan(tile_row, tile_owner, tile_sub, tile_count):
    total = tile_row.shape[0]
    owners = tile_owner[:, 0]
    index = jnp.arange(total, dtype=jnp.int32)
    z, x, y, c = my_place()
    shift = (
        (owners // 32 - z + 4) % 4 * 32
        + ((owners // 8) % 4 - x + 4) % 4 * 8
        + ((owners // 2) % 4 - y + 4) % 4 * 2
        + (owners % 2 - c + 2) % 2
    )
    k = (shift * UNSTRIDE) % DEVICES
    earlier = (owners[:, None] == owners[None, :]) & (index[None, :] < index[:, None])
    rank = jnp.any(earlier, axis=1).astype(jnp.int32)
    position = 2 * k + rank
    hot = index[:, None] == position[None, :]

    def placed(values):
        return jnp.sum(jnp.where(hot, values[None, :], 0), axis=1)

    order = placed(index)
    rhs = jnp.arange(4, dtype=jnp.int32)[None, :]
    ids = placed(tile_sub)[:, None] * 4 + rhs
    rows = placed(jnp.where(index < tile_count[0], tile_row, 1000))[:, None] * 4 + rhs
    ids = jnp.broadcast_to(ids.reshape(DEVICES, 8, 1), (DEVICES, 8, 128))
    rows = jnp.broadcast_to(rows.reshape(total * 4, 1), (total * 4, 128))
    return order, ids, rows


def per_device(tile_values, tile_row, tile_owner, tile_sub, tile_count, residual_times):
    order, ids, rows = plan(tile_row, tile_owner, tile_sub, tile_count)
    vmem = pl.BlockSpec(memory_space=pltpu.VMEM)
    update, residual = pl.pallas_call(
        kernel,
        out_shape=(
            jax.ShapeDtypeStruct((4, 4096), F32),
            jax.ShapeDtypeStruct((8, 128), F32),
        ),
        in_specs=[
            pl.BlockSpec(memory_space=pltpu.SMEM),
            pl.BlockSpec(memory_space=pl.ANY),
            vmem,
            vmem,
            vmem,
        ],
        out_specs=(vmem, vmem),
        scratch_shapes=[
            pltpu.VMEM((256, 128, 128), F32),
            pltpu.VMEM((DEVICES, 256, 256), BF16),
            pltpu.VMEM((DEVICES, 8, 128), jnp.int32),
            pltpu.VMEM((4, DEVICES, 8, 128), F32),
            pltpu.VMEM((4, DEVICES, 8, 128), F32),
            pltpu.VMEM((1024, 128), BF16),
            pltpu.VMEM((GROUPS, 128, 128), BF16),
            pltpu.VMEM((1024, 128), BF16),
            pltpu.VMEM((GROUPS, 128, 128), BF16),
            pltpu.VMEM((128, 256), F32),
            pltpu.VMEM((128, 128), F32),
            pltpu.VMEM((NORMS, 16, 8, 128), F32),
            pltpu.VMEM((NORMS, 8, 8, 128), F32),
            pltpu.VMEM((NORMS, 2, 8, 128), F32),
            pltpu.SemaphoreType.DMA((LOADS,)),
            pltpu.SemaphoreType.DMA,
            pltpu.SemaphoreType.DMA,
            pltpu.SemaphoreType.DMA((4,)),
            pltpu.SemaphoreType.DMA((4, GROUPS)),
            pltpu.SemaphoreType.DMA((NORMS,)),
            pltpu.SemaphoreType.DMA((NORMS,)),
            pltpu.SemaphoreType.DMA((NORMS,)),
            pltpu.SemaphoreType.DMA((NORMS,)),
        ],
        compiler_params=pltpu.CompilerParams(
            collective_id=0, has_side_effects=True, vmem_limit_bytes=52 * 2**20
        ),
        name="lsqr",
    )(order, tile_values, ids, rows, residual_times)
    return update, residual[0:4, 0]


def solution(mesh):
    placed = (
        P(("region", "rays"), None, None),
        P(("region", "rays")),
        P(("region", "rays"), None),
        P(("region", "rays")),
        P(("region", "rays")),
        P(None, ("region", "rays")),
    )
    return jax.shard_map(
        per_device,
        mesh=mesh,
        in_specs=placed,
        out_specs=(P(None, ("region", "rays")), P()),
        check_vma=False,
    )
```

```python
import functools

import jax
import jax.numpy as jnp
from jax import lax
from jax.experimental import pallas as pl
from jax.experimental.pallas import tpu as pltpu
from jax.sharding import PartitionSpec as P

EPSILON = 1e-06
MESH = pl.DeviceIdType.MESH
F32 = jnp.float32
BF16 = jnp.bfloat16

DEVICES = 128
GROUP = 16
GROUPS = DEVICES // GROUP
NORMS = 5
LOADS = 8


def my_place():
    z = lax.axis_index("region")
    rays = lax.axis_index("rays")
    return z, rays // 8, (rays // 2) % 4, rays % 2


def corners(sign):
    z, x, y, c = my_place()
    xs = [((x + 4 + sign * d) % 4) * 8 for d in range(4)]
    ys = [((y + 4 + sign * d) % 4) * 2 for d in range(4)]
    return [xs[i // 4] + ys[i % 4] for i in range(GROUP)]


def group_partners(g, plane, sign):
    z, x, y, c = my_place()
    zs = [(z + 4 + sign * ((g // 2 + d) % 4)) % 4 for d in range(4)]
    cs = [(c + g + d) % 2 for d in range(2)]
    return [(zs[i % 4], plane[i] + cs[(i // 4) % 2]) for i in range(GROUP)]


def split(values):
    high = values.astype(BF16)
    low = (values - high.astype(F32)).astype(BF16)
    return high, low


def dot(a, b):
    return jnp.dot(a, b, preferred_element_type=F32)


def dot_t(a, b):
    return lax.dot_general(a, b, (((1,), (1,)), ((), ())), preferred_element_type=F32)


def kernel(
    order_ref,
    tiles_ref,
    ids_ref,
    rows_ref,
    times_ref,
    update_ref,
    residual_ref,
    tiles,
    weights,
    ids_in,
    outbox,
    inbox,
    cell_pick,
    cell_sum,
    row_pick,
    row_sum,
    spread,
    prods,
    norm_a,
    norm_b,
    norm_mine,
    load_sem,
    id_send,
    id_recv,
    send_sem,
    recv_sem,
    na_send,
    na_recv,
    nb_send,
    nb_recv,
):
    z, x, y, c = my_place()
    xy = x * 4 + y
    zc = z * 2 + c
    per_load = tiles_ref.shape[0] // LOADS

    def load(i):
        where = pl.ds(i * per_load, per_load)
        return pltpu.make_async_copy(tiles_ref.at[where], tiles.at[where], load_sem.at[i])

    for i in range(LOADS):
        load(i).start()

    barrier = pltpu.get_barrier_semaphore()

    planes = {1: corners(1), -1: corners(-1)}

    def each_partner(g, sign, action):
        for i, device in enumerate(group_partners(g, planes[sign], sign)):
            if i == 0:

                @pl.when(g > 0)
                def _():
                    action(g * GROUP, device)
            else:
                action(g * GROUP + i, device)

    def greet(k, device):
        pl.semaphore_signal(barrier, inc=1, device_id=device, device_id_type=MESH)

    def send_id(k, device):
        pltpu.make_async_remote_copy(
            src_ref=ids_ref.at[k],
            dst_ref=ids_in.at[k],
            send_sem=id_send,
            recv_sem=id_recv,
            device_id=device,
            device_id_type=MESH,
        ).start()

    def all_partners(action):
        def group(g, carry):
            each_partner(g, 1, action)
            return carry

        lax.fori_loop(0, GROUPS, group, 0)

    all_partners(greet)
    pl.semaphore_wait(barrier, DEVICES - 1)
    all_partners(send_id)
    ids_in[0] = ids_ref[0]

    def norm_start(turn, part):
        norm_mine[turn, 0] = part
        norm_a[turn, xy] = part

        for d in range(1, 16):
            pltpu.make_async_remote_copy(
                src_ref=norm_mine.at[turn, 0],
                dst_ref=norm_a.at[turn, xy],
                send_sem=na_send.at[turn],
                recv_sem=na_recv.at[turn],
                device_id=(z, planes[1][d] + c),
                device_id_type=MESH,
            ).start()

    def norm_middle(turn):
        got = norm_a.at[turn, pl.ds(0, 15)]
        pltpu.make_async_copy(got, got, na_recv.at[turn]).wait()
        total = norm_a[turn, 0]
        for i in range(1, 16):
            total = total + norm_a[turn, i]
        norm_mine[turn, 1] = total
        norm_b[turn, zc] = total

        for d in range(1, 8):
            pltpu.make_async_remote_copy(
                src_ref=norm_mine.at[turn, 1],
                dst_ref=norm_b.at[turn, zc],
                send_sem=nb_send.at[turn],
                recv_sem=nb_recv.at[turn],
                device_id=((z + d // 2) % 4, planes[1][0] + (c + d) % 2),
                device_id_type=MESH,
            ).start()

    def norm_end(turn):
        got = norm_b.at[turn, pl.ds(0, 7)]
        pltpu.make_async_copy(got, got, nb_recv.at[turn]).wait()
        total = norm_b[turn, 0]
        for i in range(1, 8):
            total = total + norm_b[turn, i]
        total = total + pltpu.roll(total, 4, 0)
        total = jnp.broadcast_to(jnp.sum(total, axis=1, keepdims=True), total.shape)
        return jnp.sqrt(total + EPSILON)

    def norm_part(values):
        squares = (values * values).reshape(-1, 8, 128)
        return jnp.sum(squares, axis=0)

    def tall(scalar, values):
        return jnp.broadcast_to(scalar[None], (values.shape[0] // 8, 8, 128)).reshape(values.shape)

    def group_send(turn, g, sign):
        def one(k, device):
            pltpu.make_async_remote_copy(
                src_ref=outbox.at[turn, k],
                dst_ref=inbox.at[turn, k],
                send_sem=send_sem.at[turn],
                recv_sem=recv_sem.at[turn, g],
                device_id=device,
                device_id_type=MESH,
            ).start()

        each_partner(g, sign, one)

        @pl.when(g == 0)
        def _():
            inbox[turn, 0] = outbox[turn, 0]

    def group_wait(turn, g):
        @pl.when(g == 0)
        def _():
            got = inbox.at[turn, pl.ds(0, GROUP - 1)]
            pltpu.make_async_copy(got, got, recv_sem.at[turn, 0]).wait()

        @pl.when(g > 0)
        def _():
            got = inbox.at[turn, pl.ds(0, GROUP)]
            pltpu.make_async_copy(got, got, recv_sem.at[turn, g]).wait()

    first_half = (lax.broadcasted_iota(jnp.int32, (16, 128), 0) % 8) < 4
    first_rows = lax.broadcasted_iota(jnp.int32, (8, 128), 0) < 4

    def adjoint_send(turn, ray_vec, build):
        high, low = split(ray_vec)
        zero = jnp.zeros((64, 256), BF16)
        source = jnp.concatenate([jnp.concatenate([high, low], axis=1), zero], axis=0)

        def group(g, carry):
            here = pl.ds(g * 128, 128)
            spread[...] = dot(row_pick[here, :], source)
            for i in range(GROUP):
                k = g * GROUP + i
                if build:
                    for s in range(2):
                        tile = tiles[order_ref[2 * k + s]]
                        tile_high, tile_low = split(tile)
                        weights[k, s * 128 : (s + 1) * 128, 0:128] = tile_high
                        weights[k, s * 128 : (s + 1) * 128, 128:256] = tile_low
                both = jnp.concatenate(
                    [spread[i * 8 : i * 8 + 8, 0:128], spread[i * 8 : i * 8 + 8, 128:256]], axis=0
                )
                left = jnp.concatenate(
                    [jnp.where(first_half, both, 0.0), jnp.where(first_half, 0.0, both)], axis=1
                ).astype(BF16)
                out = dot(left, weights[k])
                out = out[:, 0:128] + out[:, 128:256]
                outbox[turn, k] = out[0:8] + out[8:16]
            group_send(turn, g, 1)

            @pl.when(g == 2)
            def _():
                norm_middle(turn)

            return carry

        lax.fori_loop(0, GROUPS, group, 0)

    def adjoint_finish(turn):
        def group(g, total):
            group_wait(turn, g)
            here = pl.multiple_of(g * 128, 128)
            arrived = inbox[turn, pl.ds(g * GROUP, GROUP)].reshape(128, 128)
            high, low = split(arrived)
            sums = cell_sum[g]
            return total + dot(
                jnp.concatenate([sums, sums], axis=1), jnp.concatenate([high, low], axis=0)
            )

        return lax.fori_loop(0, GROUPS, group, jnp.zeros((128, 128), F32))

    def forward_send(turn, model_vec):
        high, low = split(model_vec)
        source = jnp.concatenate([high, low], axis=0)

        def group(g, carry):
            picks = cell_pick[pl.ds(g * 128, 128), :]
            reply = dot(jnp.concatenate([picks, picks], axis=1), source)
            outbox[turn, pl.ds(g * GROUP, GROUP)] = reply.reshape(GROUP, 8, 128)
            group_send(turn, g, -1)
            return carry

        lax.fori_loop(0, GROUPS, group, 0)

    def forward_finish(turn):
        def group(g, total):
            group_wait(turn, g)
            for i in range(GROUP):
                k = g * GROUP + i
                high, low = split(inbox[turn, k])
                both = jnp.concatenate([high.astype(F32), low.astype(F32)], axis=0)
                left = jnp.concatenate([both, both], axis=1).astype(BF16)
                out = dot_t(left, weights[k])
                out = out[0:8] + out[8:16]
                prods[i * 8 : i * 8 + 8, :] = jnp.where(first_rows, out[:, 0:128], out[:, 128:256])
            high, low = split(prods[...])
            sums = row_sum[g]

            @pl.when(g == 0)
            def _():
                norm_middle(turn)

            return total + dot(
                jnp.concatenate([sums, sums], axis=1), jnp.concatenate([high, low], axis=0)
            )

        return lax.fori_loop(0, GROUPS, group, jnp.zeros((128, 128), F32))[0:64]

    data = jnp.concatenate([times_ref[:, b * 128 : (b + 1) * 128] for b in range(16)], axis=0)

    norm_start(0, norm_part(data))
    lanes = lax.broadcasted_iota(jnp.int32, (128, 128), 1)

    def row_marks(g, carry):
        marks = (rows_ref[pl.ds(g * 128, 128), :] == lanes).astype(F32)
        row_pick[pl.ds(g * 128, 128), :] = marks.astype(BF16)
        row_sum[g] = marks.T.astype(BF16)
        return carry

    lax.fori_loop(0, GROUPS, row_marks, 0)
    for i in range(LOADS):
        load(i).wait()

    adjoint_send(0, data, True)

    got_ids = ids_in.at[pl.ds(0, DEVICES - 1)]
    pltpu.make_async_copy(got_ids, got_ids, id_recv).wait()

    def cell_marks(g, carry):
        marks = ids_in[pl.ds(g * GROUP, GROUP)].reshape(128, 128) == lanes
        marks = marks.astype(F32)
        cell_pick[pl.ds(g * 128, 128), :] = marks.astype(BF16)
        cell_sum[g] = marks.T.astype(BF16)
        return carry

    lax.fori_loop(0, GROUPS, cell_marks, 0)

    pushed = adjoint_finish(0)
    beta_first = norm_end(0)
    ray_vec = data / tall(beta_first, data)
    pushed = pushed / tall(beta_first, pushed)

    norm_start(1, norm_part(pushed))
    forward_send(1, pushed)
    image = forward_finish(1)
    alpha = norm_end(1)
    model_vec = pushed / tall(alpha, pushed)
    direction = model_vec
    phi_bar = beta_first
    rho_bar = alpha
    image = image / tall(alpha, image) - tall(alpha, image) * ray_vec

    norm_start(2, norm_part(image))
    adjoint_send(2, image, False)
    pushed = adjoint_finish(2)
    beta = norm_end(2)
    ray_vec = image / tall(beta, image)
    pushed = pushed / tall(beta, pushed) - tall(beta, pushed) * model_vec

    norm_start(3, norm_part(pushed))
    forward_send(3, pushed)
    rho = jnp.sqrt(rho_bar * rho_bar + beta * beta)
    cosine = rho_bar / rho
    sine = beta / rho
    phi = cosine * phi_bar
    phi_bar = sine * phi_bar
    update = tall(phi / rho, direction) * direction
    image = forward_finish(3)
    alpha = norm_end(3)
    model_vec = pushed / tall(alpha, pushed)
    theta = sine * alpha
    rho_bar = -cosine * alpha
    direction = model_vec - tall(theta / rho, direction) * direction
    image = image / tall(alpha, image) - tall(alpha, image) * ray_vec

    norm_start(4, norm_part(image))
    norm_middle(4)
    beta = norm_end(4)
    rho = jnp.sqrt(rho_bar * rho_bar + beta * beta)
    cosine = rho_bar / rho
    sine = beta / rho
    phi = cosine * phi_bar
    phi_bar = sine * phi_bar
    update = update + tall(phi / rho, direction) * direction
    for b in range(32):
        update_ref[:, b * 128 : (b + 1) * 128] = update[b * 4 : b * 4 + 4, :]
    residual_ref[...] = phi_bar / beta_first

    sent = ids_in.at[pl.ds(0, DEVICES - 1)]
    pltpu.make_async_copy(sent, sent, id_send).wait()
    for turn in range(4):
        sent = outbox.at[turn, pl.ds(0, DEVICES - 1)]
        pltpu.make_async_copy(sent, sent, send_sem.at[turn]).wait()
    for turn in range(NORMS):
        sent = norm_a.at[turn, pl.ds(0, 15)]
        pltpu.make_async_copy(sent, sent, na_send.at[turn]).wait()
        sent = norm_b.at[turn, pl.ds(0, 7)]
        pltpu.make_async_copy(sent, sent, nb_send.at[turn]).wait()


def plan(tile_row, tile_owner, tile_sub, tile_count):
    total = tile_row.shape[0]
    owners = tile_owner[:, 0]
    index = jnp.arange(total, dtype=jnp.int32)
    z, x, y, c = my_place()
    dz, dx = (owners // 32 - z + 4) % 4, ((owners // 8) % 4 - x + 4) % 4
    dy, dc = ((owners // 2) % 4 - y + 4) % 4, (owners % 2 - c + 2) % 2
    g = (dz - dy + 4) % 4 * 2 + (dc + dx) % 2
    k = g * GROUP + dx * 4 + dy
    earlier = (owners[:, None] == owners[None, :]) & (index[None, :] < index[:, None])
    rank = jnp.any(earlier, axis=1).astype(jnp.int32)
    position = 2 * k + rank
    hot = index[:, None] == position[None, :]

    def placed(values):
        return jnp.sum(jnp.where(hot, values[None, :], 0), axis=1)

    order = placed(index)
    rhs = jnp.arange(4, dtype=jnp.int32)[None, :]
    ids = placed(tile_sub)[:, None] * 4 + rhs
    rows = placed(jnp.where(index < tile_count[0], tile_row, 1000))[:, None] * 4 + rhs
    ids = jnp.broadcast_to(ids.reshape(DEVICES, 8, 1), (DEVICES, 8, 128))
    rows = jnp.broadcast_to(rows.reshape(total * 4, 1), (total * 4, 128))
    return order, ids, rows


def per_device(tile_values, tile_row, tile_owner, tile_sub, tile_count, residual_times):
    order, ids, rows = plan(tile_row, tile_owner, tile_sub, tile_count)
    vmem = pl.BlockSpec(memory_space=pltpu.VMEM)
    update, residual = pl.pallas_call(
        kernel,
        out_shape=(
            jax.ShapeDtypeStruct((4, 4096), F32),
            jax.ShapeDtypeStruct((8, 128), F32),
        ),
        in_specs=[
            pl.BlockSpec(memory_space=pltpu.SMEM),
            pl.BlockSpec(memory_space=pl.ANY),
            vmem,
            vmem,
            vmem,
        ],
        out_specs=(vmem, vmem),
        scratch_shapes=[
            pltpu.VMEM((256, 128, 128), F32),
            pltpu.VMEM((DEVICES, 256, 256), BF16),
            pltpu.VMEM((DEVICES, 8, 128), jnp.int32),
            pltpu.VMEM((4, DEVICES, 8, 128), F32),
            pltpu.VMEM((4, DEVICES, 8, 128), F32),
            pltpu.VMEM((1024, 128), BF16),
            pltpu.VMEM((GROUPS, 128, 128), BF16),
            pltpu.VMEM((1024, 128), BF16),
            pltpu.VMEM((GROUPS, 128, 128), BF16),
            pltpu.VMEM((128, 256), F32),
            pltpu.VMEM((128, 128), F32),
            pltpu.VMEM((NORMS, 16, 8, 128), F32),
            pltpu.VMEM((NORMS, 8, 8, 128), F32),
            pltpu.VMEM((NORMS, 2, 8, 128), F32),
            pltpu.SemaphoreType.DMA((LOADS,)),
            pltpu.SemaphoreType.DMA,
            pltpu.SemaphoreType.DMA,
            pltpu.SemaphoreType.DMA((4,)),
            pltpu.SemaphoreType.DMA((4, GROUPS)),
            pltpu.SemaphoreType.DMA((NORMS,)),
            pltpu.SemaphoreType.DMA((NORMS,)),
            pltpu.SemaphoreType.DMA((NORMS,)),
            pltpu.SemaphoreType.DMA((NORMS,)),
        ],
        compiler_params=pltpu.CompilerParams(
            collective_id=0, has_side_effects=True, vmem_limit_bytes=52 * 2**20
        ),
        name="lsqr",
    )(order, tile_values, ids, rows, residual_times)
    return update, residual[0:4, 0]


def solution(mesh):
    placed = (
        P(("region", "rays"), None, None),
        P(("region", "rays")),
        P(("region", "rays"), None),
        P(("region", "rays")),
        P(("region", "rays")),
        P(None, ("region", "rays")),
    )
    return jax.shard_map(
        per_device,
        mesh=mesh,
        in_specs=placed,
        out_specs=(P(None, ("region", "rays")), P()),
        check_vma=False,
    )
```

```python
import functools

import jax
import jax.numpy as jnp
from jax import lax
from jax.experimental import pallas as pl
from jax.experimental.pallas import tpu as pltpu
from jax.sharding import PartitionSpec as P

EPSILON = 1e-06
MESH = pl.DeviceIdType.MESH
F32 = jnp.float32
BF16 = jnp.bfloat16

DEVICES = 128
GROUP = 16
GROUPS = DEVICES // GROUP
def distance(shift):
    hops = [shift // 32, shift // 8 % 4, shift // 2 % 4]
    return sum(min(d, 4 - d) for d in hops)


ORDER = sorted(range(DEVICES), key=lambda shift: (-distance(shift), -(shift % 2), shift))
OWN = DEVICES - 1
FORWARD_SENDS = (0, 7, 1, 6, 2, 5, 3, 4)
FORWARD_TURNS = (7, 0, 6, 1, 5, 2, 4, 3)
NORMS = 5
CHUNKS = 2
LOADS = 8


def my_place():
    z = lax.axis_index("region")
    rays = lax.axis_index("rays")
    return z, rays // 8, (rays // 2) % 4, rays % 2


def partners(sign):
    z, x, y, c = my_place()
    zs = [(z + 4 + sign * d) % 4 for d in range(4)]
    xs = [((x + 4 + sign * d) % 4) * 8 for d in range(4)]
    ys = [((y + 4 + sign * d) % 4) * 2 for d in range(4)]
    cs = [c, (c + 1) % 2]
    rays = [xs[r // 8] + ys[r // 2 % 4] + cs[r % 2] for r in range(32)]
    return [(zs[shift // 32], rays[shift % 32]) for shift in ORDER]


def split(values):
    high = values.astype(BF16)
    low = (values - high.astype(F32)).astype(BF16)
    return high, low


def dot(a, b):
    return jnp.dot(a, b, preferred_element_type=F32)


def dot_t(a, b):
    return lax.dot_general(a, b, (((1,), (1,)), ((), ())), preferred_element_type=F32)


def kernel(
    count_ref,
    tiles_ref,
    row_ref,
    owner_ref,
    sub_ref,
    times_ref,
    update_ref,
    residual_ref,
    tiles,
    weights,
    order_row,
    order,
    ids_mine,
    ids_in,
    outbox,
    inbox,
    cell_pick,
    cell_sum,
    row_pick,
    row_sum,
    spread,
    prods,
    norm_in,
    norm_mine,
    load_sem,
    order_sem,
    id_send,
    id_recv,
    send_sem,
    recv_sem,
    norm_send,
    norm_recv,
):
    z, x, y, c = my_place()
    me = z * 32 + x * 8 + y * 2 + c
    per_load = tiles_ref.shape[0] // LOADS

    def load(i):
        where = pl.ds(i * per_load, per_load)
        return pltpu.make_async_copy(tiles_ref.at[where], tiles.at[where], load_sem.at[i])

    for i in range(LOADS):
        load(i).start()

    barrier = pltpu.get_barrier_semaphore()

    devices = {1: partners(1), -1: partners(-1)}

    def greet(k, device):
        pl.semaphore_signal(barrier, inc=1, device_id=device, device_id_type=MESH)

    def send_id(k, device):
        pltpu.make_async_remote_copy(
            src_ref=ids_mine.at[k],
            dst_ref=ids_in.at[k],
            send_sem=id_send,
            recv_sem=id_recv,
            device_id=device,
            device_id_type=MESH,
        ).start()

    def all_partners(action):
        for k in range(DEVICES - 1):
            action(k, devices[1][k])

    all_partners(greet)

    sublane = lax.broadcasted_iota(jnp.int32, (8, 128), 0)
    lane = lax.broadcasted_iota(jnp.int32, (8, 128), 1)

    def norm_start(turn, part):
        total = jnp.broadcast_to(jnp.sum(part, axis=1, keepdims=True), (8, 128))
        row = jnp.sum(jnp.where(lane % 8 == sublane, total, 0.0), axis=0, keepdims=True)
        norm_mine[turn] = row
        norm_in[turn, me] = row

    def send_norm(turn, device):
        pltpu.make_async_remote_copy(
            src_ref=norm_mine.at[turn],
            dst_ref=norm_in.at[turn, me],
            send_sem=norm_send.at[turn],
            recv_sem=norm_recv.at[turn],
            device_id=device,
            device_id_type=MESH,
        ).start()

    def norm_end(turn):
        got = norm_in.at[turn, pl.ds(0, DEVICES - 1)]
        pltpu.make_async_copy(got, got, norm_recv.at[turn]).wait()
        row = jnp.sum(norm_in[turn], axis=0)
        mine = (lane < 8) & (lane % 4 == sublane % 4)
        total = jnp.sum(
            jnp.where(mine, jnp.broadcast_to(row, (8, 128)), 0.0), axis=1, keepdims=True
        )
        return jnp.sqrt(jnp.broadcast_to(total, (8, 128)) + EPSILON)

    def norm_part(values):
        squares = (values * values).reshape(-1, 8, 128)
        return jnp.sum(squares, axis=0)

    def tall(scalar, values):
        return jnp.broadcast_to(scalar[None], (values.shape[0] // 8, 8, 128)).reshape(values.shape)

    def group_send(turn, g, sign):
        def one(k, device):
            send_norm(turn, device)
            if turn == 0:
                send_id(k, device)
            pltpu.make_async_remote_copy(
                src_ref=outbox.at[turn, k],
                dst_ref=inbox.at[turn, k],
                send_sem=send_sem.at[turn],
                recv_sem=recv_sem.at[turn, g],
                device_id=device,
                device_id_type=MESH,
            ).start()

        for k in range(g * GROUP, (g + 1) * GROUP):
            if k != OWN:
                one(k, devices[sign][k])

        if g == GROUPS - 1:
            inbox[turn, OWN] = outbox[turn, OWN]

    def group_wait(turn, g):
        got = inbox.at[turn, pl.ds(0, GROUP - 1 if g == GROUPS - 1 else GROUP)]
        pltpu.make_async_copy(got, got, recv_sem.at[turn, g]).wait()

    first_half = (lax.broadcasted_iota(jnp.int32, (16, 128), 0) % 8) < 4
    first_rows = lax.broadcasted_iota(jnp.int32, (8, 128), 0) < 4

    def adjoint_send(turn, ray_vec, build):
        high, low = split(ray_vec)
        zero = jnp.zeros((64, 256), BF16)
        source = jnp.concatenate([jnp.concatenate([high, low], axis=1), zero], axis=0)

        spread[...] = dot(row_pick[...], source)

        def group(g):
            for i in range(GROUP):
                k = g * GROUP + i
                if build:
                    for s in range(2):
                        tile = tiles[order[0, 2 * k + s]]
                        tile_high, tile_low = split(tile)
                        weights[k, s * 128 : (s + 1) * 128, 0:128] = tile_high
                        weights[k, s * 128 : (s + 1) * 128, 128:256] = tile_low
                both = jnp.concatenate(
                    [spread[pl.ds(k * 8, 8), 0:128], spread[pl.ds(k * 8, 8), 128:256]], axis=0
                )
                left = jnp.concatenate(
                    [jnp.where(first_half, both, 0.0), jnp.where(first_half, 0.0, both)], axis=1
                ).astype(BF16)
                out = dot(left, weights[k])
                out = out[:, 0:128] + out[:, 128:256]
                outbox[turn, k] = out[0:8] + out[8:16]

        for g in range(GROUPS):
            group(g)
            if build and g == 0:
                pl.semaphore_wait(barrier, DEVICES - 1)
            group_send(turn, g, 1)

    def adjoint_finish(turn):
        total = jnp.zeros((128, 128), F32)
        for chunk in range(CHUNKS):
            first = chunk * GROUPS // CHUNKS
            for g in range(first, first + GROUPS // CHUNKS):
                group_wait(turn, g)
            arrived = inbox[turn, first * GROUP : (first + GROUPS // CHUNKS) * GROUP]
            high, low = split(arrived.reshape(-1, 128))
            sums = cell_sum[:, first * 128 : (first + GROUPS // CHUNKS) * 128]
            total = total + dot(sums, high) + dot(sums, low)
        return total

    def forward_send(turn, model_vec):
        high, low = split(model_vec)
        source = jnp.concatenate([high, low], axis=0)

        picks = cell_pick[...]
        reply = dot(jnp.concatenate([picks, picks], axis=1), source)
        outbox[turn] = reply.reshape(DEVICES, 8, 128)

        for g in FORWARD_SENDS:
            group_send(turn, g, -1)

    def forward_finish(turn):
        for g in FORWARD_TURNS:
            group_wait(turn, g)
            for i in range(GROUP):
                k = g * GROUP + i
                arrived = inbox[turn, k]
                high = arrived.astype(BF16).astype(F32)
                both = jnp.concatenate([high, arrived - high], axis=0)
                left = jnp.concatenate([both, both], axis=1).astype(BF16)
                out = dot_t(left, weights[k])
                out = out[0:8] + out[8:16]
                prods[pl.ds(k * 8, 8), :] = jnp.where(first_rows, out[:, 0:128], out[:, 128:256])
        high, low = split(prods[...])
        sums = row_sum[...]
        return dot(sums, high) + dot(sums, low)

    data = jnp.concatenate([times_ref[:, b * 128 : (b + 1) * 128] for b in range(16)], axis=0)

    norm_start(0, norm_part(data))
    lanes = lax.broadcasted_iota(jnp.int32, (128, 128), 1)

    owner = owner_ref[...]
    shift = (
        (((owner >> 5) - z) & 3) * 32
        + (((owner >> 3) - x) & 3) * 8
        + (((owner >> 1) - y) & 3) * 2
        + ((owner - c) & 1)
    )
    tile_lane = lax.broadcasted_iota(jnp.int32, (128, 256), 1)
    tile_sublane = lax.broadcasted_iota(jnp.int32, (128, 256), 0)

    def upright(row, half):
        column = jnp.broadcast_to(row[:, half * 128 : half * 128 + 128], (128, 128)).T
        return jnp.concatenate([column, column], axis=1)

    rank = jnp.zeros((1, 256), jnp.int32)
    for half in range(2):
        earlier = (upright(owner, half) == owner) & (tile_sublane + half * 128 < tile_lane)
        rank = rank + jnp.sum(earlier.astype(jnp.int32), axis=0, keepdims=True)
    code = shift * 2 + rank
    lane_row = tile_lane[0:1]
    keys = jnp.zeros((1, 256), jnp.int32)
    for k in range(DEVICES):
        keys = jnp.where(lane_row >> 1 == k, ORDER[k] * 2, keys)
    keys = keys + (lane_row & 1)
    found = jnp.zeros((1, 256), jnp.int32)
    for half in range(2):
        hit = upright(code, half) == keys
        found = found + jnp.sum(
            jnp.where(hit, tile_sublane + half * 128, 0), axis=0, keepdims=True
        )
    order_row[...] = found
    to_scalars = pltpu.make_async_copy(order_row, order, order_sem)
    to_scalars.start()

    live_row = jnp.where(lane_row < count_ref[0], row_ref[...], 31)
    payload = (live_row + 32 * sub_ref[...]).astype(F32)
    slot = lax.broadcasted_iota(jnp.int32, (8, 256), 0) >> 2
    for g in range(GROUPS):
        for i in range(GROUP):
            k = g * GROUP + i
            hit = code == slot + 2 * ORDER[k]
            value = jnp.sum(jnp.where(hit, payload, 0.0), axis=1, keepdims=True)
            value = jnp.broadcast_to(value, (8, 128)).astype(jnp.int32)
            marks = ((value & 31) * 4 + (sublane & 3) == lane).astype(F32)
            spread[i * 8 : i * 8 + 8, 0:128] = marks
            cells = (value >> 5 == lane >> 2).astype(jnp.int32)
            ids_mine[k] = cells[0:1] + 2 * cells[4:5]
        marks = spread[0:128, 0:128]
        row_pick[g * 128 : g * 128 + 128, :] = marks.astype(BF16)
        row_sum[:, g * 128 : g * 128 + 128] = marks.T[0:64].astype(BF16)
    ids_in[OWN] = ids_mine[OWN]
    to_scalars.wait()
    for i in range(LOADS):
        load(i).wait()

    adjoint_send(0, data, True)

    got_ids = ids_in.at[pl.ds(0, DEVICES - 1)]
    pltpu.make_async_copy(got_ids, got_ids, id_recv).wait()

    def cell_marks(g, carry):
        for i in range(GROUP):
            code = jnp.broadcast_to(ids_in[g * GROUP + i], (8, 128))
            hit = (code == sublane // 4 + 1) | (code == 3)
            marks = (hit & (lane % 4 == sublane % 4)).astype(F32)
            spread[i * 8 : i * 8 + 8, 0:128] = marks
        marks = spread[0:128, 0:128]
        cell_pick[pl.ds(g * 128, 128), :] = marks.astype(BF16)
        cell_sum[:, pl.ds(pl.multiple_of(g * 128, 128), 128)] = marks.T.astype(BF16)
        return carry

    lax.fori_loop(0, GROUPS, cell_marks, 0)

    pushed = adjoint_finish(0)
    beta_first = norm_end(0)
    ray_vec = data / tall(beta_first, data)
    pushed = pushed / tall(beta_first, pushed)

    norm_start(1, norm_part(pushed))
    forward_send(1, pushed)
    image = forward_finish(1)
    alpha = norm_end(1)
    model_vec = pushed / tall(alpha, pushed)
    direction = model_vec
    phi_bar = beta_first
    rho_bar = alpha
    image = image / tall(alpha, image) - tall(alpha, image) * ray_vec

    norm_start(2, norm_part(image))
    adjoint_send(2, image, False)
    pushed = adjoint_finish(2)
    beta = norm_end(2)
    ray_vec = image / tall(beta, image)
    pushed = pushed / tall(beta, pushed) - tall(beta, pushed) * model_vec

    norm_start(3, norm_part(pushed))
    forward_send(3, pushed)
    rho = jnp.sqrt(rho_bar * rho_bar + beta * beta)
    cosine = rho_bar / rho
    sine = beta / rho
    phi = cosine * phi_bar
    phi_bar = sine * phi_bar
    update = tall(phi / rho, direction) * direction
    image = forward_finish(3)
    alpha = norm_end(3)
    model_vec = pushed / tall(alpha, pushed)
    theta = sine * alpha
    rho_bar = -cosine * alpha
    direction = model_vec - tall(theta / rho, direction) * direction
    image = image / tall(alpha, image) - tall(alpha, image) * ray_vec

    norm_start(4, norm_part(image))
    all_partners(lambda k, device: send_norm(4, device))
    beta = norm_end(4)
    rho = jnp.sqrt(rho_bar * rho_bar + beta * beta)
    cosine = rho_bar / rho
    sine = beta / rho
    phi = cosine * phi_bar
    phi_bar = sine * phi_bar
    update = update + tall(phi / rho, direction) * direction
    for b in range(32):
        update_ref[:, b * 128 : (b + 1) * 128] = update[b * 4 : b * 4 + 4, :]
    residual_ref[...] = phi_bar / beta_first

    sent = ids_in.at[pl.ds(0, DEVICES - 1)]
    pltpu.make_async_copy(sent, sent, id_send).wait()
    for turn in range(4):
        sent = outbox.at[turn, pl.ds(0, DEVICES - 1)]
        pltpu.make_async_copy(sent, sent, send_sem.at[turn]).wait()
    for turn in range(NORMS):
        sent = norm_in.at[turn, pl.ds(0, DEVICES - 1)]
        pltpu.make_async_copy(sent, sent, norm_send.at[turn]).wait()


def per_device(tile_values, tile_row, tile_owner, tile_sub, tile_count, residual_times):
    tiles = tile_row.shape[0]
    vmem = pl.BlockSpec(memory_space=pltpu.VMEM)
    update, residual = pl.pallas_call(
        kernel,
        out_shape=(
            jax.ShapeDtypeStruct((4, 4096), F32),
            jax.ShapeDtypeStruct((8, 128), F32),
        ),
        in_specs=[
            pl.BlockSpec(memory_space=pltpu.SMEM),
            pl.BlockSpec(memory_space=pl.ANY),
            vmem,
            vmem,
            vmem,
            vmem,
        ],
        out_specs=(vmem, vmem),
        scratch_shapes=[
            pltpu.VMEM((256, 128, 128), F32),
            pltpu.VMEM((DEVICES, 256, 256), BF16),
            pltpu.VMEM((1, 256), jnp.int32),
            pltpu.SMEM((1, 256), jnp.int32),
            pltpu.VMEM((DEVICES, 1, 128), jnp.int32),
            pltpu.VMEM((DEVICES, 1, 128), jnp.int32),
            pltpu.VMEM((4, DEVICES, 8, 128), F32),
            pltpu.VMEM((4, DEVICES, 8, 128), F32),
            pltpu.VMEM((1024, 128), BF16),
            pltpu.VMEM((128, 1024), BF16),
            pltpu.VMEM((1024, 128), BF16),
            pltpu.VMEM((64, 1024), BF16),
            pltpu.VMEM((1024, 256), F32),
            pltpu.VMEM((1024, 128), F32),
            pltpu.VMEM((NORMS, DEVICES, 1, 128), F32),
            pltpu.VMEM((NORMS, 1, 128), F32),
            pltpu.SemaphoreType.DMA((LOADS,)),
            pltpu.SemaphoreType.DMA,
            pltpu.SemaphoreType.DMA,
            pltpu.SemaphoreType.DMA,
            pltpu.SemaphoreType.DMA((4,)),
            pltpu.SemaphoreType.DMA((4, GROUPS)),
            pltpu.SemaphoreType.DMA((NORMS,)),
            pltpu.SemaphoreType.DMA((NORMS,)),
        ],
        compiler_params=pltpu.CompilerParams(
            collective_id=0, has_side_effects=True, vmem_limit_bytes=52 * 2**20
        ),
        name="lsqr",
    )(
        tile_count,
        tile_values,
        tile_row.reshape(1, tiles),
        tile_owner.reshape(1, tiles),
        tile_sub.reshape(1, tiles),
        residual_times,
    )
    return update, residual[0:4, 0]


def solution(mesh):
    placed = (
        P(("region", "rays"), None, None),
        P(("region", "rays")),
        P(("region", "rays"), None),
        P(("region", "rays")),
        P(("region", "rays")),
        P(None, ("region", "rays")),
    )
    return jax.shard_map(
        per_device,
        mesh=mesh,
        in_specs=placed,
        out_specs=(P(None, ("region", "rays")), P()),
        check_vma=False,
    )
```

```python
import functools

import jax
import jax.numpy as jnp
from jax import lax
from jax.experimental import pallas as pl
from jax.experimental.pallas import tpu as pltpu
from jax.sharding import PartitionSpec as P

EPSILON = 1e-06
MESH = pl.DeviceIdType.MESH
F32 = jnp.float32
BF16 = jnp.bfloat16

DEVICES = 128
GROUP = 16
GROUPS = DEVICES // GROUP
def distance(shift):
    hops = [shift // 32, shift // 8 % 4, shift // 2 % 4]
    return sum(min(d, 4 - d) for d in hops)


ORDER = sorted(range(DEVICES), key=lambda shift: (-distance(shift), -(shift % 2), shift))
OWN = DEVICES - 1
FORWARD_SENDS = (0, 7, 1, 6, 2, 5, 3, 4)
FORWARD_TURNS = (7, 0, 6, 1, 5, 2, 4, 3)
NORMS = 5
CHUNKS = 2
LOADS = 8


def my_place():
    z = lax.axis_index("region")
    rays = lax.axis_index("rays")
    return z, rays // 8, (rays // 2) % 4, rays % 2


def partners(sign):
    z, x, y, c = my_place()
    zs = [(z + 4 + sign * d) % 4 for d in range(4)]
    xs = [((x + 4 + sign * d) % 4) * 8 for d in range(4)]
    ys = [((y + 4 + sign * d) % 4) * 2 for d in range(4)]
    cs = [c, (c + 1) % 2]
    rays = [xs[r // 8] + ys[r // 2 % 4] + cs[r % 2] for r in range(32)]
    return [(zs[shift // 32], rays[shift % 32]) for shift in ORDER]


def split(values):
    high = values.astype(BF16)
    low = (values - high.astype(F32)).astype(BF16)
    return high, low


def dot(a, b):
    return jnp.dot(a, b, preferred_element_type=F32)


def dot_t(a, b):
    return lax.dot_general(a, b, (((1,), (1,)), ((), ())), preferred_element_type=F32)


def kernel(
    count_ref,
    tiles_ref,
    places_ref,
    times_ref,
    update_ref,
    residual_ref,
    tiles,
    weights,
    order_row,
    order,
    ids_mine,
    ids_in,
    outbox,
    inbox,
    cell_pick,
    cell_sum,
    row_pick,
    row_sum,
    spread,
    prods,
    norm_in,
    norm_mine,
    load_sem,
    order_sem,
    id_send,
    id_recv,
    send_sem,
    recv_sem,
    norm_send,
    norm_recv,
):
    z, x, y, c = my_place()
    me = z * 32 + x * 8 + y * 2 + c
    per_load = tiles_ref.shape[0] // LOADS

    def load(i):
        where = pl.ds(i * per_load, per_load)
        return pltpu.make_async_copy(tiles_ref.at[where], tiles.at[where], load_sem.at[i])

    for i in range(LOADS):
        load(i).start()

    barrier = pltpu.get_barrier_semaphore()

    devices = {1: partners(1), -1: partners(-1)}

    def greet(k, device):
        pl.semaphore_signal(barrier, inc=1, device_id=device, device_id_type=MESH)

    def send_id(k, device):
        pltpu.make_async_remote_copy(
            src_ref=ids_mine.at[k],
            dst_ref=ids_in.at[k],
            send_sem=id_send,
            recv_sem=id_recv,
            device_id=device,
            device_id_type=MESH,
        ).start()

    def all_partners(action):
        for k in range(DEVICES - 1):
            action(k, devices[1][k])

    all_partners(greet)

    sublane = lax.broadcasted_iota(jnp.int32, (8, 128), 0)
    lane = lax.broadcasted_iota(jnp.int32, (8, 128), 1)

    def norm_start(turn, part):
        total = jnp.broadcast_to(jnp.sum(part, axis=1, keepdims=True), (8, 128))
        row = jnp.sum(jnp.where(lane % 8 == sublane, total, 0.0), axis=0, keepdims=True)
        norm_mine[turn] = row
        norm_in[turn, me] = row

    def send_norm(turn, device):
        pltpu.make_async_remote_copy(
            src_ref=norm_mine.at[turn],
            dst_ref=norm_in.at[turn, me],
            send_sem=norm_send.at[turn],
            recv_sem=norm_recv.at[turn],
            device_id=device,
            device_id_type=MESH,
        ).start()

    def norm_end(turn):
        got = norm_in.at[turn, pl.ds(0, DEVICES - 1)]
        pltpu.make_async_copy(got, got, norm_recv.at[turn]).wait()
        row = jnp.sum(norm_in[turn], axis=0)
        mine = (lane < 8) & (lane % 4 == sublane % 4)
        total = jnp.sum(
            jnp.where(mine, jnp.broadcast_to(row, (8, 128)), 0.0), axis=1, keepdims=True
        )
        return jnp.sqrt(jnp.broadcast_to(total, (8, 128)) + EPSILON)

    def norm_part(values):
        squares = (values * values).reshape(-1, 8, 128)
        return jnp.sum(squares, axis=0)

    def tall(scalar, values):
        return jnp.broadcast_to(scalar[None], (values.shape[0] // 8, 8, 128)).reshape(values.shape)

    def group_send(turn, g, sign):
        def one(k, device):
            send_norm(turn, device)
            if turn == 0:
                send_id(k, device)
            pltpu.make_async_remote_copy(
                src_ref=outbox.at[turn, k],
                dst_ref=inbox.at[turn, k],
                send_sem=send_sem.at[turn],
                recv_sem=recv_sem.at[turn, g],
                device_id=device,
                device_id_type=MESH,
            ).start()

        for k in range(g * GROUP, (g + 1) * GROUP):
            if k != OWN:
                one(k, devices[sign][k])

        if g == GROUPS - 1:
            inbox[turn, OWN] = outbox[turn, OWN]

    def group_wait(turn, g):
        got = inbox.at[turn, pl.ds(0, GROUP - 1 if g == GROUPS - 1 else GROUP)]
        pltpu.make_async_copy(got, got, recv_sem.at[turn, g]).wait()

    first_half = (lax.broadcasted_iota(jnp.int32, (16, 128), 0) % 8) < 4
    first_rows = lax.broadcasted_iota(jnp.int32, (8, 128), 0) < 4

    def adjoint_send(turn, ray_vec, build):
        high, low = split(ray_vec)
        zero = jnp.zeros((64, 256), BF16)
        source = jnp.concatenate([jnp.concatenate([high, low], axis=1), zero], axis=0)

        spread[...] = dot(row_pick[...], source)

        def group(g):
            for i in range(GROUP):
                k = g * GROUP + i
                if build:
                    for s in range(2):
                        tile = tiles[order[0, 2 * k + s]]
                        tile_high, tile_low = split(tile)
                        weights[k, s * 128 : (s + 1) * 128, 0:128] = tile_high
                        weights[k, s * 128 : (s + 1) * 128, 128:256] = tile_low
                both = jnp.concatenate(
                    [spread[pl.ds(k * 8, 8), 0:128], spread[pl.ds(k * 8, 8), 128:256]], axis=0
                )
                left = jnp.concatenate(
                    [jnp.where(first_half, both, 0.0), jnp.where(first_half, 0.0, both)], axis=1
                ).astype(BF16)
                out = dot(left, weights[k])
                out = out[:, 0:128] + out[:, 128:256]
                outbox[turn, k] = out[0:8] + out[8:16]

        for g in range(GROUPS):
            group(g)
            if build and g == 0:
                pl.semaphore_wait(barrier, DEVICES - 1)
            group_send(turn, g, 1)

    def adjoint_finish(turn):
        total = jnp.zeros((128, 128), F32)
        for chunk in range(CHUNKS):
            first = chunk * GROUPS // CHUNKS
            for g in range(first, first + GROUPS // CHUNKS):
                group_wait(turn, g)
            arrived = inbox[turn, first * GROUP : (first + GROUPS // CHUNKS) * GROUP]
            high, low = split(arrived.reshape(-1, 128))
            sums = cell_sum[:, first * 128 : (first + GROUPS // CHUNKS) * 128]
            total = total + dot(sums, high) + dot(sums, low)
        return total

    def forward_send(turn, model_vec):
        high, low = split(model_vec)
        source = jnp.concatenate([high, low], axis=0)

        picks = cell_pick[...]
        reply = dot(jnp.concatenate([picks, picks], axis=1), source)
        outbox[turn] = reply.reshape(DEVICES, 8, 128)

        for g in FORWARD_SENDS:
            group_send(turn, g, -1)

    def forward_finish(turn):
        for g in FORWARD_TURNS:
            group_wait(turn, g)
            for i in range(GROUP):
                k = g * GROUP + i
                arrived = inbox[turn, k]
                high = arrived.astype(BF16).astype(F32)
                both = jnp.concatenate([high, arrived - high], axis=0)
                left = jnp.concatenate([both, both], axis=1).astype(BF16)
                out = dot_t(left, weights[k])
                out = out[0:8] + out[8:16]
                prods[pl.ds(k * 8, 8), :] = jnp.where(first_rows, out[:, 0:128], out[:, 128:256])
        high, low = split(prods[...])
        sums = row_sum[...]
        return dot(sums, high) + dot(sums, low)

    data = jnp.concatenate([times_ref[:, b * 128 : (b + 1) * 128] for b in range(16)], axis=0)

    norm_start(0, norm_part(data))
    lanes = lax.broadcasted_iota(jnp.int32, (128, 128), 1)

    places = places_ref[...]
    owner = places >> 9
    shift = (
        (((owner >> 5) - z) & 3) * 32
        + (((owner >> 3) - x) & 3) * 8
        + (((owner >> 1) - y) & 3) * 2
        + ((owner - c) & 1)
    )
    tile_lane = lax.broadcasted_iota(jnp.int32, (128, 256), 1)
    tile_sublane = lax.broadcasted_iota(jnp.int32, (128, 256), 0)

    def upright(row, half):
        column = jnp.broadcast_to(row[:, half * 128 : half * 128 + 128], (128, 128)).T
        return jnp.concatenate([column, column], axis=1)

    rank = jnp.zeros((1, 256), jnp.int32)
    for half in range(2):
        earlier = (upright(owner, half) == owner) & (tile_sublane + half * 128 < tile_lane)
        rank = rank + jnp.sum(earlier.astype(jnp.int32), axis=0, keepdims=True)
    code = shift * 2 + rank
    lane_row = tile_lane[0:1]
    keys = jnp.zeros((1, 256), jnp.int32)
    for k in range(DEVICES):
        keys = jnp.where(lane_row >> 1 == k, ORDER[k] * 2, keys)
    keys = keys + (lane_row & 1)
    found = jnp.zeros((1, 256), jnp.int32)
    for half in range(2):
        hit = upright(code, half) == keys
        found = found + jnp.sum(
            jnp.where(hit, tile_sublane + half * 128, 0), axis=0, keepdims=True
        )
    order_row[...] = found
    to_scalars = pltpu.make_async_copy(order_row, order, order_sem)
    to_scalars.start()

    live_row = jnp.where(lane_row < count_ref[0], places & 15, 31)
    payload = (live_row + 32 * ((places >> 4) & 31)).astype(F32)
    slot = lax.broadcasted_iota(jnp.int32, (8, 256), 0) >> 2
    for g in range(GROUPS):
        for i in range(GROUP):
            k = g * GROUP + i
            hit = code == slot + 2 * ORDER[k]
            value = jnp.sum(jnp.where(hit, payload, 0.0), axis=1, keepdims=True)
            value = jnp.broadcast_to(value, (8, 128)).astype(jnp.int32)
            marks = ((value & 31) * 4 + (sublane & 3) == lane).astype(F32)
            spread[i * 8 : i * 8 + 8, 0:128] = marks
            cells = (value >> 5 == lane >> 2).astype(jnp.int32)
            ids_mine[k] = cells[0:1] + 2 * cells[4:5]
        marks = spread[0:128, 0:128]
        row_pick[g * 128 : g * 128 + 128, :] = marks.astype(BF16)
        row_sum[:, g * 128 : g * 128 + 128] = marks.T[0:64].astype(BF16)
    ids_in[OWN] = ids_mine[OWN]
    to_scalars.wait()
    for i in range(LOADS):
        load(i).wait()

    adjoint_send(0, data, True)

    got_ids = ids_in.at[pl.ds(0, DEVICES - 1)]
    pltpu.make_async_copy(got_ids, got_ids, id_recv).wait()

    def cell_marks(g, carry):
        for i in range(GROUP):
            code = jnp.broadcast_to(ids_in[g * GROUP + i], (8, 128))
            hit = (code == sublane // 4 + 1) | (code == 3)
            marks = (hit & (lane % 4 == sublane % 4)).astype(F32)
            spread[i * 8 : i * 8 + 8, 0:128] = marks
        marks = spread[0:128, 0:128]
        cell_pick[pl.ds(g * 128, 128), :] = marks.astype(BF16)
        cell_sum[:, pl.ds(pl.multiple_of(g * 128, 128), 128)] = marks.T.astype(BF16)
        return carry

    lax.fori_loop(0, GROUPS, cell_marks, 0)

    pushed = adjoint_finish(0)
    beta_first = norm_end(0)
    ray_vec = data / tall(beta_first, data)
    pushed = pushed / tall(beta_first, pushed)

    norm_start(1, norm_part(pushed))
    forward_send(1, pushed)
    image = forward_finish(1)
    alpha = norm_end(1)
    model_vec = pushed / tall(alpha, pushed)
    direction = model_vec
    phi_bar = beta_first
    rho_bar = alpha
    image = image / tall(alpha, image) - tall(alpha, image) * ray_vec

    norm_start(2, norm_part(image))
    adjoint_send(2, image, False)
    pushed = adjoint_finish(2)
    beta = norm_end(2)
    ray_vec = image / tall(beta, image)
    pushed = pushed / tall(beta, pushed) - tall(beta, pushed) * model_vec

    norm_start(3, norm_part(pushed))
    forward_send(3, pushed)
    rho = jnp.sqrt(rho_bar * rho_bar + beta * beta)
    cosine = rho_bar / rho
    sine = beta / rho
    phi = cosine * phi_bar
    phi_bar = sine * phi_bar
    update = tall(phi / rho, direction) * direction
    image = forward_finish(3)
    alpha = norm_end(3)
    model_vec = pushed / tall(alpha, pushed)
    theta = sine * alpha
    rho_bar = -cosine * alpha
    direction = model_vec - tall(theta / rho, direction) * direction
    image = image / tall(alpha, image) - tall(alpha, image) * ray_vec

    norm_start(4, norm_part(image))
    all_partners(lambda k, device: send_norm(4, device))
    beta = norm_end(4)
    rho = jnp.sqrt(rho_bar * rho_bar + beta * beta)
    cosine = rho_bar / rho
    sine = beta / rho
    phi = cosine * phi_bar
    phi_bar = sine * phi_bar
    update = update + tall(phi / rho, direction) * direction
    for b in range(32):
        update_ref[:, b * 128 : (b + 1) * 128] = update[b * 4 : b * 4 + 4, :]
    residual_ref[...] = phi_bar / beta_first

    sent = ids_in.at[pl.ds(0, DEVICES - 1)]
    pltpu.make_async_copy(sent, sent, id_send).wait()
    for turn in range(4):
        sent = outbox.at[turn, pl.ds(0, DEVICES - 1)]
        pltpu.make_async_copy(sent, sent, send_sem.at[turn]).wait()
    for turn in range(NORMS):
        sent = norm_in.at[turn, pl.ds(0, DEVICES - 1)]
        pltpu.make_async_copy(sent, sent, norm_send.at[turn]).wait()


def per_device(tile_values, tile_row, tile_owner, tile_sub, tile_count, residual_times):
    tiles = tile_row.shape[0]
    vmem = pl.BlockSpec(memory_space=pltpu.VMEM)
    update, residual = pl.pallas_call(
        kernel,
        out_shape=(
            jax.ShapeDtypeStruct((4, 4096), F32),
            jax.ShapeDtypeStruct((8, 128), F32),
        ),
        in_specs=[
            pl.BlockSpec(memory_space=pltpu.SMEM),
            pl.BlockSpec(memory_space=pl.ANY),
            vmem,
            vmem,
        ],
        out_specs=(vmem, vmem),
        scratch_shapes=[
            pltpu.VMEM((256, 128, 128), F32),
            pltpu.VMEM((DEVICES, 256, 256), BF16),
            pltpu.VMEM((1, 256), jnp.int32),
            pltpu.SMEM((1, 256), jnp.int32),
            pltpu.VMEM((DEVICES, 1, 128), jnp.int32),
            pltpu.VMEM((DEVICES, 1, 128), jnp.int32),
            pltpu.VMEM((4, DEVICES, 8, 128), F32),
            pltpu.VMEM((4, DEVICES, 8, 128), F32),
            pltpu.VMEM((1024, 128), BF16),
            pltpu.VMEM((128, 1024), BF16),
            pltpu.VMEM((1024, 128), BF16),
            pltpu.VMEM((64, 1024), BF16),
            pltpu.VMEM((1024, 256), F32),
            pltpu.VMEM((1024, 128), F32),
            pltpu.VMEM((NORMS, DEVICES, 1, 128), F32),
            pltpu.VMEM((NORMS, 1, 128), F32),
            pltpu.SemaphoreType.DMA((LOADS,)),
            pltpu.SemaphoreType.DMA,
            pltpu.SemaphoreType.DMA,
            pltpu.SemaphoreType.DMA,
            pltpu.SemaphoreType.DMA((4,)),
            pltpu.SemaphoreType.DMA((4, GROUPS)),
            pltpu.SemaphoreType.DMA((NORMS,)),
            pltpu.SemaphoreType.DMA((NORMS,)),
        ],
        compiler_params=pltpu.CompilerParams(
            collective_id=0, has_side_effects=True, vmem_limit_bytes=52 * 2**20
        ),
        name="lsqr",
    )(
        tile_count,
        tile_values,
        (tile_row + 16 * tile_sub + 512 * tile_owner[:, 0]).reshape(1, tiles),
        residual_times,
    )
    return update, residual[0:4, 0]


def solution(mesh):
    placed = (
        P(("region", "rays"), None, None),
        P(("region", "rays")),
        P(("region", "rays"), None),
        P(("region", "rays")),
        P(("region", "rays")),
        P(None, ("region", "rays")),
    )
    return jax.shard_map(
        per_device,
        mesh=mesh,
        in_specs=placed,
        out_specs=(P(None, ("region", "rays")), P()),
        check_vma=False,
    )
```

```python
import functools

import jax
import jax.numpy as jnp
from jax import lax
from jax.experimental import pallas as pl
from jax.experimental.pallas import tpu as pltpu
from jax.sharding import PartitionSpec as P

EPSILON = 1e-06
MESH = pl.DeviceIdType.MESH
F32 = jnp.float32
BF16 = jnp.bfloat16

DEVICES = 128
GROUP = 16
GROUPS = DEVICES // GROUP
def distance(shift):
    hops = [shift // 32, shift // 8 % 4, shift // 2 % 4]
    return sum(min(d, 4 - d) for d in hops)


ORDER = sorted(range(DEVICES), key=lambda shift: (-distance(shift), -(shift % 2), shift))
OWN = DEVICES - 1
FORWARD_SENDS = (0, 7, 1, 6, 2, 5, 3, 4)
FORWARD_TURNS = (7, 0, 6, 1, 5, 2, 4, 3)
NORMS = 5
CHUNKS = 2
LOADS = 8


def my_place():
    z = lax.axis_index("region")
    rays = lax.axis_index("rays")
    return z, rays // 8, (rays // 2) % 4, rays % 2


def partners(sign):
    z, x, y, c = my_place()
    zs = [(z + 4 + sign * d) % 4 for d in range(4)]
    xs = [((x + 4 + sign * d) % 4) * 8 for d in range(4)]
    ys = [((y + 4 + sign * d) % 4) * 2 for d in range(4)]
    cs = [c, (c + 1) % 2]
    rays = [xs[r // 8] + ys[r // 2 % 4] + cs[r % 2] for r in range(32)]
    return [(zs[shift // 32], rays[shift % 32]) for shift in ORDER]


def split(values):
    high = values.astype(BF16)
    low = (values - high.astype(F32)).astype(BF16)
    return high, low


def dot(a, b):
    return jnp.dot(a, b, preferred_element_type=F32)


def dot_t(a, b):
    return lax.dot_general(a, b, (((1,), (1,)), ((), ())), preferred_element_type=F32)


def kernel(
    count_ref,
    tiles_ref,
    places_ref,
    times_ref,
    update_ref,
    residual_ref,
    tiles,
    weights,
    order_row,
    order,
    ids_mine,
    ids_in,
    outbox,
    inbox,
    cell_pick,
    cell_sum,
    row_pick,
    row_sum,
    spread,
    prods,
    norm_in,
    norm_mine,
    load_sem,
    order_sem,
    id_send,
    id_recv,
    send_sem,
    recv_sem,
    norm_send,
    norm_recv,
):
    z, x, y, c = my_place()
    me = z * 32 + x * 8 + y * 2 + c
    per_load = tiles_ref.shape[0] // LOADS

    def load(i):
        where = pl.ds(i * per_load, per_load)
        return pltpu.make_async_copy(tiles_ref.at[where], tiles.at[where], load_sem.at[i])

    for i in range(LOADS):
        load(i).start()

    barrier = pltpu.get_barrier_semaphore()

    devices = {1: partners(1), -1: partners(-1)}

    def greet(k, device):
        pl.semaphore_signal(barrier, inc=1, device_id=device, device_id_type=MESH)

    def send_id(k, device):
        pltpu.make_async_remote_copy(
            src_ref=ids_mine.at[k],
            dst_ref=ids_in.at[k],
            send_sem=id_send,
            recv_sem=id_recv,
            device_id=device,
            device_id_type=MESH,
        ).start()

    def all_partners(action):
        for k in range(DEVICES - 1):
            action(k, devices[1][k])

    all_partners(greet)

    sublane = lax.broadcasted_iota(jnp.int32, (8, 128), 0)
    lane = lax.broadcasted_iota(jnp.int32, (8, 128), 1)

    def norm_start(turn, part):
        total = jnp.broadcast_to(jnp.sum(part, axis=1, keepdims=True), (8, 128))
        row = jnp.sum(jnp.where(lane % 8 == sublane, total, 0.0), axis=0, keepdims=True)
        norm_mine[turn] = row
        norm_in[turn, me] = row

    def send_norm(turn, device):
        pltpu.make_async_remote_copy(
            src_ref=norm_mine.at[turn],
            dst_ref=norm_in.at[turn, me],
            send_sem=norm_send.at[turn],
            recv_sem=norm_recv.at[turn],
            device_id=device,
            device_id_type=MESH,
        ).start()

    def norm_end(turn):
        got = norm_in.at[turn, pl.ds(0, DEVICES - 1)]
        pltpu.make_async_copy(got, got, norm_recv.at[turn]).wait()
        row = jnp.sum(norm_in[turn], axis=0)
        mine = (lane < 8) & (lane % 4 == sublane % 4)
        total = jnp.sum(
            jnp.where(mine, jnp.broadcast_to(row, (8, 128)), 0.0), axis=1, keepdims=True
        )
        return jnp.sqrt(jnp.broadcast_to(total, (8, 128)) + EPSILON)

    def norm_part(values):
        squares = (values * values).reshape(-1, 8, 128)
        return jnp.sum(squares, axis=0)

    def tall(scalar, values):
        return jnp.broadcast_to(scalar[None], (values.shape[0] // 8, 8, 128)).reshape(values.shape)

    def group_send(turn, g, sign):
        def one(k, device):
            if sign > 0:
                send_norm(turn, device)
            if turn == 0:
                send_id(k, device)
            pltpu.make_async_remote_copy(
                src_ref=outbox.at[turn, k],
                dst_ref=inbox.at[turn, k],
                send_sem=send_sem.at[turn],
                recv_sem=recv_sem.at[turn, g],
                device_id=device,
                device_id_type=MESH,
            ).start()

        for k in range(g * GROUP, (g + 1) * GROUP):
            if k != OWN:
                one(k, devices[sign][k])

        if g == GROUPS - 1:
            inbox[turn, OWN] = outbox[turn, OWN]

    def group_wait(turn, g):
        got = inbox.at[turn, pl.ds(0, GROUP - 1 if g == GROUPS - 1 else GROUP)]
        pltpu.make_async_copy(got, got, recv_sem.at[turn, g]).wait()

    first_half = (lax.broadcasted_iota(jnp.int32, (16, 128), 0) % 8) < 4
    first_rows = lax.broadcasted_iota(jnp.int32, (8, 128), 0) < 4

    def adjoint_send(turn, ray_vec, build):
        high, low = split(ray_vec)
        zero = jnp.zeros((64, 256), BF16)
        source = jnp.concatenate([jnp.concatenate([high, low], axis=1), zero], axis=0)

        spread[...] = dot(row_pick[...], source)

        def group(g):
            for i in range(GROUP):
                k = g * GROUP + i
                if build:
                    for s in range(2):
                        tile = tiles[order[0, 2 * k + s]]
                        tile_high, tile_low = split(tile)
                        weights[k, s * 128 : (s + 1) * 128, 0:128] = tile_high
                        weights[k, s * 128 : (s + 1) * 128, 128:256] = tile_low
                both = jnp.concatenate(
                    [spread[pl.ds(k * 8, 8), 0:128], spread[pl.ds(k * 8, 8), 128:256]], axis=0
                )
                left = jnp.concatenate(
                    [jnp.where(first_half, both, 0.0), jnp.where(first_half, 0.0, both)], axis=1
                ).astype(BF16)
                out = dot(left, weights[k])
                out = out[:, 0:128] + out[:, 128:256]
                outbox[turn, k] = out[0:8] + out[8:16]

        for g in range(GROUPS):
            group(g)
            if build and g == 0:
                pl.semaphore_wait(barrier, DEVICES - 1)
            group_send(turn, g, 1)

    def adjoint_finish(turn):
        total = jnp.zeros((128, 128), F32)
        for chunk in range(CHUNKS):
            first = chunk * GROUPS // CHUNKS
            for g in range(first, first + GROUPS // CHUNKS):
                group_wait(turn, g)
            arrived = inbox[turn, first * GROUP : (first + GROUPS // CHUNKS) * GROUP]
            high, low = split(arrived.reshape(-1, 128))
            sums = cell_sum[:, first * 128 : (first + GROUPS // CHUNKS) * 128]
            total = total + dot(sums, high) + dot(sums, low)
        return total

    def forward_send(turn, model_vec):
        high, low = split(model_vec)
        source = jnp.concatenate([high, low], axis=0)

        picks = cell_pick[...]
        reply = dot(jnp.concatenate([picks, picks], axis=1), source)
        outbox[turn] = reply.reshape(DEVICES, 8, 128)

        for g in FORWARD_SENDS:
            group_send(turn, g, -1)
        all_partners(lambda k, device: send_norm(turn, device))

    def forward_finish(turn):
        for g in FORWARD_TURNS:
            group_wait(turn, g)
            for i in range(GROUP):
                k = g * GROUP + i
                arrived = inbox[turn, k]
                high = arrived.astype(BF16).astype(F32)
                both = jnp.concatenate([high, arrived - high], axis=0)
                left = jnp.concatenate([both, both], axis=1).astype(BF16)
                out = dot_t(left, weights[k])
                out = out[0:8] + out[8:16]
                prods[pl.ds(k * 8, 8), :] = jnp.where(first_rows, out[:, 0:128], out[:, 128:256])
        high, low = split(prods[...])
        sums = row_sum[...]
        return dot(sums, high) + dot(sums, low)

    data = jnp.concatenate([times_ref[:, b * 128 : (b + 1) * 128] for b in range(16)], axis=0)

    norm_start(0, norm_part(data))
    lanes = lax.broadcasted_iota(jnp.int32, (128, 128), 1)

    places = places_ref[...]
    owner = places >> 9
    shift = (
        (((owner >> 5) - z) & 3) * 32
        + (((owner >> 3) - x) & 3) * 8
        + (((owner >> 1) - y) & 3) * 2
        + ((owner - c) & 1)
    )
    tile_lane = lax.broadcasted_iota(jnp.int32, (128, 256), 1)
    tile_sublane = lax.broadcasted_iota(jnp.int32, (128, 256), 0)

    def upright(row, half):
        column = jnp.broadcast_to(row[:, half * 128 : half * 128 + 128], (128, 128)).T
        return jnp.concatenate([column, column], axis=1)

    rank = jnp.zeros((1, 256), jnp.int32)
    for half in range(2):
        earlier = (upright(owner, half) == owner) & (tile_sublane + half * 128 < tile_lane)
        rank = rank + jnp.sum(earlier.astype(jnp.int32), axis=0, keepdims=True)
    code = shift * 2 + rank
    lane_row = tile_lane[0:1]
    keys = jnp.zeros((1, 256), jnp.int32)
    for k in range(DEVICES):
        keys = jnp.where(lane_row >> 1 == k, ORDER[k] * 2, keys)
    keys = keys + (lane_row & 1)
    found = jnp.zeros((1, 256), jnp.int32)
    for half in range(2):
        hit = upright(code, half) == keys
        found = found + jnp.sum(
            jnp.where(hit, tile_sublane + half * 128, 0), axis=0, keepdims=True
        )
    order_row[...] = found
    to_scalars = pltpu.make_async_copy(order_row, order, order_sem)
    to_scalars.start()

    live_row = jnp.where(lane_row < count_ref[0], places & 15, 31)
    payload = (live_row + 32 * ((places >> 4) & 31)).astype(F32)
    slot = lax.broadcasted_iota(jnp.int32, (8, 256), 0) >> 2
    for g in range(GROUPS):
        for i in range(GROUP):
            k = g * GROUP + i
            hit = code == slot + 2 * ORDER[k]
            value = jnp.sum(jnp.where(hit, payload, 0.0), axis=1, keepdims=True)
            value = jnp.broadcast_to(value, (8, 128)).astype(jnp.int32)
            marks = ((value & 31) * 4 + (sublane & 3) == lane).astype(F32)
            spread[i * 8 : i * 8 + 8, 0:128] = marks
            cells = (value >> 5 == lane >> 2).astype(jnp.int32)
            ids_mine[k] = cells[0:1] + 2 * cells[4:5]
        marks = spread[0:128, 0:128]
        row_pick[g * 128 : g * 128 + 128, :] = marks.astype(BF16)
        row_sum[:, g * 128 : g * 128 + 128] = marks.T[0:64].astype(BF16)
    ids_in[OWN] = ids_mine[OWN]
    to_scalars.wait()
    for i in range(LOADS):
        load(i).wait()

    adjoint_send(0, data, True)

    got_ids = ids_in.at[pl.ds(0, DEVICES - 1)]
    pltpu.make_async_copy(got_ids, got_ids, id_recv).wait()

    def cell_marks(g, carry):
        for i in range(GROUP):
            code = jnp.broadcast_to(ids_in[g * GROUP + i], (8, 128))
            hit = (code == sublane // 4 + 1) | (code == 3)
            marks = (hit & (lane % 4 == sublane % 4)).astype(F32)
            spread[i * 8 : i * 8 + 8, 0:128] = marks
        marks = spread[0:128, 0:128]
        cell_pick[pl.ds(g * 128, 128), :] = marks.astype(BF16)
        cell_sum[:, pl.ds(pl.multiple_of(g * 128, 128), 128)] = marks.T.astype(BF16)
        return carry

    lax.fori_loop(0, GROUPS, cell_marks, 0)

    pushed = adjoint_finish(0)
    beta_first = norm_end(0)
    ray_vec = data / tall(beta_first, data)
    pushed = pushed / tall(beta_first, pushed)

    norm_start(1, norm_part(pushed))
    forward_send(1, pushed)
    image = forward_finish(1)
    alpha = norm_end(1)
    model_vec = pushed / tall(alpha, pushed)
    direction = model_vec
    phi_bar = beta_first
    rho_bar = alpha
    image = image / tall(alpha, image) - tall(alpha, image) * ray_vec

    norm_start(2, norm_part(image))
    adjoint_send(2, image, False)
    pushed = adjoint_finish(2)
    beta = norm_end(2)
    ray_vec = image / tall(beta, image)
    pushed = pushed / tall(beta, pushed) - tall(beta, pushed) * model_vec

    norm_start(3, norm_part(pushed))
    forward_send(3, pushed)
    rho = jnp.sqrt(rho_bar * rho_bar + beta * beta)
    cosine = rho_bar / rho
    sine = beta / rho
    phi = cosine * phi_bar
    phi_bar = sine * phi_bar
    update = tall(phi / rho, direction) * direction
    image = forward_finish(3)
    alpha = norm_end(3)
    model_vec = pushed / tall(alpha, pushed)
    theta = sine * alpha
    rho_bar = -cosine * alpha
    direction = model_vec - tall(theta / rho, direction) * direction
    image = image / tall(alpha, image) - tall(alpha, image) * ray_vec

    norm_start(4, norm_part(image))
    all_partners(lambda k, device: send_norm(4, device))
    beta = norm_end(4)
    rho = jnp.sqrt(rho_bar * rho_bar + beta * beta)
    cosine = rho_bar / rho
    sine = beta / rho
    phi = cosine * phi_bar
    phi_bar = sine * phi_bar
    update = update + tall(phi / rho, direction) * direction
    for b in range(32):
        update_ref[:, b * 128 : (b + 1) * 128] = update[b * 4 : b * 4 + 4, :]
    residual_ref[...] = phi_bar / beta_first

    sent = ids_in.at[pl.ds(0, DEVICES - 1)]
    pltpu.make_async_copy(sent, sent, id_send).wait()
    for turn in range(4):
        sent = outbox.at[turn, pl.ds(0, DEVICES - 1)]
        pltpu.make_async_copy(sent, sent, send_sem.at[turn]).wait()
    for turn in range(NORMS):
        sent = norm_in.at[turn, pl.ds(0, DEVICES - 1)]
        pltpu.make_async_copy(sent, sent, norm_send.at[turn]).wait()


def per_device(tile_values, tile_row, tile_owner, tile_sub, tile_count, residual_times):
    tiles = tile_row.shape[0]
    vmem = pl.BlockSpec(memory_space=pltpu.VMEM)
    update, residual = pl.pallas_call(
        kernel,
        out_shape=(
            jax.ShapeDtypeStruct((4, 4096), F32),
            jax.ShapeDtypeStruct((8, 128), F32),
        ),
        in_specs=[
            pl.BlockSpec(memory_space=pltpu.SMEM),
            pl.BlockSpec(memory_space=pl.ANY),
            vmem,
            vmem,
        ],
        out_specs=(vmem, vmem),
        scratch_shapes=[
            pltpu.VMEM((256, 128, 128), F32),
            pltpu.VMEM((DEVICES, 256, 256), BF16),
            pltpu.VMEM((1, 256), jnp.int32),
            pltpu.SMEM((1, 256), jnp.int32),
            pltpu.VMEM((DEVICES, 1, 128), jnp.int32),
            pltpu.VMEM((DEVICES, 1, 128), jnp.int32),
            pltpu.VMEM((4, DEVICES, 8, 128), F32),
            pltpu.VMEM((4, DEVICES, 8, 128), F32),
            pltpu.VMEM((1024, 128), BF16),
            pltpu.VMEM((128, 1024), BF16),
            pltpu.VMEM((1024, 128), BF16),
            pltpu.VMEM((64, 1024), BF16),
            pltpu.VMEM((1024, 256), F32),
            pltpu.VMEM((1024, 128), F32),
            pltpu.VMEM((NORMS, DEVICES, 1, 128), F32),
            pltpu.VMEM((NORMS, 1, 128), F32),
            pltpu.SemaphoreType.DMA((LOADS,)),
            pltpu.SemaphoreType.DMA,
            pltpu.SemaphoreType.DMA,
            pltpu.SemaphoreType.DMA,
            pltpu.SemaphoreType.DMA((4,)),
            pltpu.SemaphoreType.DMA((4, GROUPS)),
            pltpu.SemaphoreType.DMA((NORMS,)),
            pltpu.SemaphoreType.DMA((NORMS,)),
        ],
        compiler_params=pltpu.CompilerParams(
            collective_id=0, has_side_effects=True, vmem_limit_bytes=52 * 2**20
        ),
        name="lsqr",
    )(
        tile_count,
        tile_values,
        (tile_row + 16 * tile_sub + 512 * tile_owner[:, 0]).reshape(1, tiles),
        residual_times,
    )
    return update, residual[0:4, 0]


def solution(mesh):
    placed = (
        P(("region", "rays"), None, None),
        P(("region", "rays")),
        P(("region", "rays"), None),
        P(("region", "rays")),
        P(("region", "rays")),
        P(None, ("region", "rays")),
    )
    return jax.shard_map(
        per_device,
        mesh=mesh,
        in_specs=placed,
        out_specs=(P(None, ("region", "rays")), P()),
        check_vma=False,
    )
```
